128 devices in a mesh: group: 8 (over y, core), sub: 16 (over z, x).
Axes of the slice: x: 4, y: 4, z: 4, core: 2. Of those that a mesh axis runs over, the one named last changes fastest.
Arguments:
- current: float32 [16, 786432], P(None, ('group', 'sub')), may hold values from -6 to 6
- previous: float32 [16, 786432], P(None, ('group', 'sub')), may hold values from -6 to 6
- prev_coupling: float32 [16, 16], replicated, may hold values from -3 to 3
- mass_diag: float32 [786432], P(('group', 'sub')), may hold values from 1 to 2
- near_blocks: bfloat16 [6144, 8, 128, 128], P(('group', 'sub')), may hold values from -0.1875 to 0.1875
- near_cols: int32 [6144, 8], P(('group', 'sub')), may hold values from 0 to 6143, as said below
- cluster_basis: bfloat16 [6144, 24, 128], P(('group', 'sub')), may hold values from -0.5 to 0.5
- coupling: bfloat16 [6144, 24, 768], P(('group', 'sub')), may hold values from -0.21875 to 0.21875
- send_list: int32 [128, 128, 12], P(('group', 'sub')), may hold values from -1 to 47, as said below
- far_slot: int32 [6144, 32], P(('group', 'sub')), may hold values from 0 to 1535, as said below
Outputs:
- next_block: float32 [16, 786432], P(None, ('group', 'sub'))
- projection: float32 [16, 16], replicated
- triangle: float32 [16, 16], replicated
The draws below stay inside these ranges and needn't reach their ends.
Inputs may be any that keep to these rules, and one draw needn't show every extreme that they name: near_cols[r, 0] = r; the other near column clusters of a row are distinct, differ from r, and lie on the row cluster's device or on the devices just before or after it in the order of group then sub, taken round the ends. `send_list`: for each source and destination the live slots come first, 1 to 12 of them; every source fills all 12 slots for one destination. `far_slot`: each entry names a live slot that its source sends to the row cluster's device.
All inputs are finite; a program needn't handle non-finite values.
Results may differ from the reference program's by a relative error of at most 0.002.
Values may be sent and summed in bfloat16 or wider, within the bound.
A program may use at most 128 MiB of HBM per device.

```python
import jax
import jax.numpy as jnp
from jax import lax

NRHS = 16
CL = 128
RANK = 24
NNEAR = 8
NFAR = 32
CAP = 12
CPD = 48
NCL = 6144
N = 786432
DEVICES = 128


def route_tables(key):
    first, second, third = jax.random.split(key, 3)
    counts = jax.random.randint(first, (DEVICES, DEVICES), 1, CAP + 1)
    filled = jax.random.randint(second, (DEVICES,), 0, DEVICES)
    columns = jnp.arange(DEVICES, dtype=jnp.int32)[None, :]
    counts = jnp.where(columns == filled[:, None], CAP, counts)
    cluster_ids = jax.random.randint(third, (DEVICES, DEVICES, CAP), 0, CPD)
    live = jnp.arange(CAP, dtype=jnp.int32)[None, None, :] < counts[:, :, None]
    table = jnp.where(live, cluster_ids, -1)
    return (counts.astype(jnp.int32), table.astype(jnp.int32))


def draw_send_list(key, part):
    counts, table = route_tables(key)
    return table


def draw_far_slot(key, part):
    counts, table = route_tables(key)
    key = jax.random.fold_in(key, 7)
    first, second = jax.random.split(key)
    target = (jnp.arange(NCL, dtype=jnp.int32) // CPD)[:, None]
    source = jax.random.randint(first, (NCL, NFAR), 0, DEVICES)
    raw_draw = jax.random.randint(second, (NCL, NFAR), 0, 1048576)
    slot_index = raw_draw % counts[source, target]
    return (source * CAP + slot_index).astype(jnp.int32)


def draw_near_cols(key, part):
    key = jax.random.fold_in(key, 11)
    row_ids = jnp.arange(NCL, dtype=jnp.int32)
    owner = row_ids // CPD
    own_place = CPD + row_ids % CPD
    keys = jax.random.split(key, NCL)
    orders = jax.vmap(lambda single: jax.random.permutation(single, 3 * CPD - 1))(keys)[:, :NNEAR - 1]
    picks = orders + (orders >= own_place[:, None]).astype(jnp.int32)
    window = jnp.concatenate([own_place[:, None], picks], axis=1)
    return (((owner[:, None] - 1) * CPD + window) % NCL).astype(jnp.int32)


def level_of(rng, dims, cuts, smallest, high):
    loudness, own = 1.0, jax.random.fold_in(rng, 6)
    for axis_at, shards_of in cuts:
        steps = jnp.exp(jax.random.uniform(jax.random.fold_in(own, axis_at), (shards_of,), jnp.float32, smallest / len(cuts), high / len(cuts)))
        loudness = loudness * jnp.repeat(steps, dims[axis_at] // shards_of).reshape([-1 if axis == axis_at else 1 for axis in range(len(dims))])
    return loudness


def scatter_about(rng, extent, width, bound, cuts=(), kind=jnp.bfloat16):
    entries = width * jax.random.normal(rng, extent, jnp.float32)
    if cuts:
        entries = entries * level_of(rng, extent, cuts, -0.22, 0.18)
    return jnp.clip(entries, -bound, bound).astype(kind)


def setup_inputs(seed: int = 0) -> dict:
    seeds = jax.random.split(jax.random.key(seed), 11)
    current = scatter_about(seeds[0], (NRHS, N), 1.0, 6.0, ((1, 128),), jnp.float32)
    previous = scatter_about(seeds[1], (NRHS, N), 1.0, 6.0, ((1, 128),), jnp.float32)
    prev_coupling = scatter_about(seeds[2], (NRHS, NRHS), 0.5, 3.0, (), jnp.float32)
    mass_diag = jnp.clip(1.0 + 1.0 * jax.random.uniform(seeds[3], (N,), jnp.float32) ** level_of(seeds[3], (N,), ((0, 128),), -0.2, 0.2), 1.0, 2.0)
    near_blocks = scatter_about(seeds[4], (NCL, NNEAR, CL, CL), (NNEAR * CL) ** -0.5, 0.1875, ((0, 128),))
    near_cols = draw_near_cols(jax.random.fold_in(seeds[10], 71), 0)
    cluster_basis = scatter_about(seeds[6], (NCL, RANK, CL), CL ** -0.5, 0.5, ((0, 128),))
    coupling = scatter_about(seeds[7], (NCL, RANK, NFAR * RANK), (NFAR * RANK) ** -0.5, 0.21875, ((0, 128),))
    send_list = draw_send_list(jax.random.fold_in(seeds[10], 71), 0)
    far_slot = draw_far_slot(jax.random.fold_in(seeds[10], 71), 0)
    return {"current": current, "previous": previous, "prev_coupling": prev_coupling, "mass_diag": mass_diag, "near_blocks": near_blocks, "near_cols": near_cols, "cluster_basis": cluster_basis, "coupling": coupling, "send_list": send_list, "far_slot": far_slot}


def reference(current, previous, prev_coupling, mass_diag, near_blocks, near_cols, cluster_basis, coupling, send_list, far_slot):
    highest = lax.Precision.HIGHEST
    rhs_count = current.shape[0]
    cluster_count = near_cols.shape[0]
    current_lo = current.astype(jnp.bfloat16)
    blocks = current_lo.reshape(rhs_count, cluster_count, CL)
    coefficients = jnp.einsum('ckb,scb->cks', cluster_basis.astype(jnp.float32), blocks.astype(jnp.float32), precision=highest)
    coefficients = coefficients.reshape(cluster_count, RANK * rhs_count)
    source = far_slot // CAP
    slot_index = far_slot % CAP
    target = (jnp.arange(cluster_count, dtype=jnp.int32) // CPD)[:, None]
    local_ids = send_list[source, target, slot_index]
    columns = source * CPD + local_ids
    picked = coefficients[columns].reshape(cluster_count, NFAR * RANK, rhs_count)
    combined = jnp.einsum('rkm,rms->rks', coupling.astype(jnp.float32), picked, precision=highest)
    combined_lo = combined.astype(jnp.bfloat16)
    far_part = jnp.einsum('rka,rks->sra', cluster_basis.astype(jnp.float32), combined_lo.astype(jnp.float32), precision=highest)
    far_part = far_part.reshape(rhs_count, cluster_count * CL)

    def one_device(device):
        start = (device * CPD).astype(jnp.int32)
        tiles = lax.dynamic_slice_in_dim(near_blocks, start, CPD, 0).astype(jnp.float32)
        col_ids = lax.dynamic_slice_in_dim(near_cols, start, CPD, 0)
        gathered = blocks[:, col_ids].astype(jnp.float32)
        return jnp.einsum('rjab,srjb->sra', tiles, gathered, precision=highest)
    pieces = lax.map(one_device, jnp.arange(cluster_count // CPD, dtype=jnp.int32))
    near_part = jnp.transpose(pieces, (1, 0, 2, 3)).reshape(rhs_count, cluster_count * CL)
    image = near_part + far_part + mass_diag[None, :] * current
    total = float(current.shape[1])
    projection = jnp.dot(current, image.T, precision=highest) / total
    resid = image - jnp.dot(projection.T, current, precision=highest) - jnp.dot(prev_coupling, previous, precision=highest)
    gram = jnp.dot(resid, resid.T, precision=highest) / total
    triangle = jnp.linalg.cholesky(gram)
    next_block = lax.linalg.triangular_solve(triangle, resid, left_side=True, lower=True)
    return (next_block, projection, triangle)
```

```python
import functools

import jax
import jax.numpy as jnp
from jax import lax
from jax.experimental import pallas as pl
from jax.experimental.pallas import tpu as pltpu
from jax.sharding import PartitionSpec as P

MESH = pl.DeviceIdType.MESH
BF = jnp.bfloat16
F32 = jnp.float32
NRHS = 16
CL = 128
RANK = 24
NNEAR = 8
NFAR = 32
CAP = 12
CPD = 48
NCL = 6144
N = 786432
ROWS = CPD * CL
NGRP = CPD // 8
HIGHEST = lax.Precision.HIGHEST
PART_ROWS = (64, 64, 32)
ORDERS = ((0, 1, 2), (2, 0, 1), (1, 2, 0))
OFFSETS = (2, 1, 3)
NEAR_CHUNKS = 6


def nt(a, b, precision=None):
    return lax.dot_general(
        a, b, (((1,), (1,)), ((), ())), preferred_element_type=F32, precision=precision
    )


def tn(a, b, precision=None):
    return lax.dot_general(
        a, b, (((0,), (0,)), ((), ())), preferred_element_type=F32, precision=precision
    )


def nn(a, b, precision=None):
    return lax.dot_general(
        a, b, (((1,), (0,)), ((), ())), preferred_element_type=F32, precision=precision
    )


def split(x):
    hi = x.astype(BF)
    return hi, (x - hi.astype(F32)).astype(BF)


def kernel(
    cur_h, prev_h, pc_ref, mass_h, near_h, ncol_ref, basis_h, coup_h, slist_ref, far_ref,
    out_ref, proj_ref, tri_ref,
    cur_v, prev_v, mass_v, near_v, basis_v, coup_v,
    win, stack, jbuf, parts_a, parts_b, parts_c, table, xbuf,
    ncol_v, far_v, addr_v, ncol_s, far_s, addr_s,
    red_c, red_t,
    load_sem, near_sem, smem_sem,
    ag_send, ag_recv, sib_send, sib_recv, halo_send, halo_recv, red_send, red_recv,
):
    grp = lax.axis_index("group")
    sub = lax.axis_index("sub")
    me = grp * 16 + sub
    core = grp % 2
    pos = (sub % 4, grp // 2, sub // 4)

    def place(x, y, z, c):
        return (y * 2 + c, z * 4 + x)

    def shifted(axis, off):
        at = list(pos)
        at[axis] = (at[axis] + off) % 4
        return place(*at, core)

    sibling = place(*pos, 1 - core)

    def neighbour(off):
        d = (me + off) % 128
        return (d // 16, d % 16)

    loads = []
    for n, (src, dst) in enumerate(
        ((cur_h, cur_v), (basis_h, basis_v), (prev_h, prev_v), (mass_h, mass_v), (coup_h, coup_v))
    ):
        copy = pltpu.make_async_copy(src, dst, load_sem.at[n])
        copy.start()
        loads.append(copy)
    per = CPD * NNEAR // NEAR_CHUNKS
    near_loads = []
    for n in range(NEAR_CHUNKS):
        part = pl.ds(n * per, per)
        copy = pltpu.make_async_copy(near_h.at[part], near_v.at[part], near_sem.at[n])
        copy.start()
        near_loads.append(copy)

    peers = [shifted(a, o) for a in range(3) for o in OFFSETS]
    peers += [sibling, neighbour(1), neighbour(127)]
    barrier = pltpu.get_barrier_semaphore()
    for d in peers:
        pl.semaphore_signal(barrier, inc=1, device_id=d, device_id_type=MESH)

    wanted = ncol_ref[...] - (me - 1) * CPD
    wanted = jnp.where(wanted < 0, wanted + NCL, wanted)
    wanted = jnp.where(wanted >= NCL, wanted - NCL, wanted)
    ncol_v[:, 0:CPD] = jnp.clip(wanted, 0, 3 * CPD - 1)
    q = far_ref[...]
    src = (q * 43691) >> 19
    slot = q - src * CAP
    src_g, src_s = src >> 4, src & 15
    order = (src_g & 1) * 64 + (src_s & 3) * 16 + (src_s >> 2) * 4 + (src_g >> 1)
    far_v[:, 0:CPD] = jnp.clip(order * 16 + slot, 0, 2047)
    ncol_copy = pltpu.make_async_copy(ncol_v, ncol_s, smem_sem.at[0])
    far_copy = pltpu.make_async_copy(far_v, far_s, smem_sem.at[1])
    ncol_copy.start()
    far_copy.start()

    loads[0].wait()

    def window_step(c, _):
        cols = pl.ds(pl.multiple_of(c * CL, CL), CL)
        hi, lo = split(cur_v[:, cols])
        win[CPD + c] = hi
        stack[32:48, cols] = hi
        stack[48:64, cols] = lo
        return 0

    lax.fori_loop(0, CPD, window_step, 0, unroll=4)
    loads[1].wait()
    diag = lax.broadcasted_iota(jnp.int32, (8 * RANK, 128), 0) // RANK == (
        lax.broadcasted_iota(jnp.int32, (8 * RANK, 128), 1) // NRHS
    )
    coefs = []
    for g in range(NGRP):
        cl = win[CPD + 8 * g : CPD + 8 * g + 8].reshape(128, CL)
        y = nt(basis_v[192 * g : 192 * g + 192, :], cl)
        y = jnp.where(diag, y, 0.0).reshape(8, RANK, 128)
        coefs.append(jnp.sum(y, axis=0))
    coefs = jnp.concatenate(coefs, axis=0).astype(BF)
    slist = jnp.concatenate([slist_ref[...].astype(F32), jnp.zeros((4, 128), F32)], axis=0)
    slist = slist.astype(BF)
    bufs = (parts_a, parts_b, parts_c)

    def block(p, phase, off):
        at = [pos[a] for a in ORDERS[p]]
        at[phase] = (at[phase] + off) % 4
        return bufs[p].at[(core, at[2], at[1], at[0])[: 4 - phase]]

    own = [tuple(pos[a] for a in ORDERS[p]) for p in range(3)]
    i1, i2, i3 = own[0]
    parts_a[core, i3, i2, i1] = coefs[0:64]
    i1, i2, i3 = own[1]
    parts_b[core, i3, i2, i1] = coefs[64:128]
    i1, i2, i3 = own[2]
    parts_c[core, i3, i2, i1] = jnp.concatenate([coefs[128:144], slist], axis=0)

    pl.semaphore_wait(barrier, len(peers))

    sends = []

    def put(src_ref, dst_ref, send_sem, recv_sem, device):
        copy = pltpu.make_async_remote_copy(
            src_ref=src_ref, dst_ref=dst_ref, send_sem=send_sem, recv_sem=recv_sem,
            device_id=device, device_id_type=MESH,
        )
        copy.start()
        sends.append(copy)
        return copy

    def gather_phase(phase):
        copies = []
        for k, off in enumerate(OFFSETS):
            for p in range(3):
                n = (phase * 3 + p) * 3 + k
                ref = block(p, phase, 0)
                copies.append(
                    put(ref, ref, ag_send.at[n], ag_recv.at[n], shifted(ORDERS[p][phase], off))
                )
        return copies

    sib_copies = []

    def to_sibling(ref):
        n = len(sib_copies)
        sib_copies.append(put(ref, ref, sib_send.at[n], sib_recv.at[n], sibling))

    phase1 = gather_phase(0)
    mid = win.at[pl.ds(CPD, CPD)]
    halo = [
        put(mid, win.at[pl.ds(0, CPD)], halo_send.at[0], halo_recv.at[0], neighbour(1)),
        put(mid, win.at[pl.ds(2 * CPD, CPD)], halo_send.at[1], halo_recv.at[1], neighbour(127)),
    ]
    loads[2].wait()
    pc = pc_ref[...]
    pc_hi, pc_lo = split(pc)
    pc_rows = jnp.concatenate([pc_hi, pc_hi], axis=1)
    pc_rows2 = jnp.concatenate([pc_lo, pc_lo], axis=1)
    pc_all = jnp.concatenate([pc_rows, pc_rows2], axis=0)

    def previous_step(c, _):
        cols = pl.ds(pl.multiple_of(c * 512, 512), 512)
        hi, lo = split(prev_v[:, cols])
        stack[64:80, cols] = hi
        stack[80:96, cols] = lo
        both = nn(pc_all, jnp.concatenate([hi, lo], axis=0))
        jbuf[:, cols] = -(both[0:16] + both[16:32])
        return 0

    lax.fori_loop(0, ROWS // 512, previous_step, 0)

    for copy in phase1:
        copy.wait_recv()
    phase2 = gather_phase(1)
    loads[3].wait()
    loads[4].wait()
    for copy in phase2:
        copy.wait_recv()
    phase3 = gather_phase(2)
    for p in range(3):
        to_sibling(block(p, 2, 0))

    ncol_copy.wait()
    for copy in halo:
        copy.wait_recv()

    def near_step(r, _):
        xs, ms = [], []
        for j in range(NNEAR):
            w = ncol_s[j, r]
            xs.append(win[w])
        x = jnp.concatenate(xs, axis=1)
        m = near_v[pl.ds(r * NNEAR, NNEAR)]
        m = jnp.concatenate([m[j] for j in range(NNEAR)], axis=1)
        cols = pl.ds(pl.multiple_of(r * CL, CL), CL)
        jbuf[:, cols] += nt(x, m) + mass_v[pl.ds(r, 1), :] * cur_v[:, cols]
        return 0

    rows_per = CPD // NEAR_CHUNKS
    for n in range(NEAR_CHUNKS):
        near_loads[n].wait()
        lax.fori_loop(n * rows_per, (n + 1) * rows_per, near_step, 0)

    for copy in phase3:
        copy.wait_recv()
    for p in range(3):
        for off in (1, 2, 3):
            to_sibling(block(p, 2, off))
    far_copy.wait()
    for copy in sib_copies:
        copy.wait_recv()

    def table_step(t, _):
        c, x, z, y = t // 64, t // 16 % 4, t // 4 % 4, t % 4
        table[pl.ds(t * 18, 8)] = parts_a[c, z, y, x].astype(F32).reshape(8, 8, 128)
        table[pl.ds(t * 18 + 8, 8)] = parts_b[c, y, x, z].astype(F32).reshape(8, 8, 128)
        table[pl.ds(t * 18 + 16, 2)] = parts_c[c, x, z, y, 0:16].astype(F32).reshape(2, 8, 128)
        return 0

    lax.fori_loop(0, 128, table_step, 0)

    lists = parts_c[:, :, :, :, 16:32].reshape(128 * 16, 128)
    mine = (lax.broadcasted_iota(jnp.int32, (16, 128), 1) == me).astype(BF)
    local = nt(mine, lists)
    row_id = lax.broadcasted_iota(jnp.int32, (16, 128), 0)
    lane_id = lax.broadcasted_iota(jnp.int32, (16, 128), 1)
    picked = jnp.zeros((16, 128), F32)
    for i in range(16):
        picked = jnp.where(row_id == i, local[:, i * 128 : (i + 1) * 128], picked)
    picked = jnp.clip(picked.astype(jnp.int32), 0, CPD - 1)
    first = (row_id * 8 + (lane_id >> 4)) * 18 + (picked >> 3) * 3
    addr_v[...] = jnp.clip(first * 8 + (picked & 7), 0, (128 * 18 - 3) * 8 + 7)
    addr_copy = pltpu.make_async_copy(addr_v, addr_s, smem_sem.at[2])
    addr_copy.start()
    addr_copy.wait()

    lane_block = lax.broadcasted_iota(jnp.int32, (RANK, 128), 1) // NRHS

    def far_step(g, _):
        def pick_step(jj, _):
            halves = []
            for k in range(2):
                total = None
                for r in range(8):
                    at = far_s[jj * 2 + k, g * 8 + r]
                    word = addr_s[at >> 7, at & 127]
                    rows = table[pl.ds(word >> 3, 3)].reshape(RANK, 128)
                    rows = pltpu.roll(rows, ((r - word) & 7) * NRHS, 1)
                    total = rows if r == 0 else jnp.where(lane_block == r, rows, total)
                halves.append(total)
            both = jnp.concatenate(halves, axis=0).astype(BF)
            xbuf[pl.ds(pl.multiple_of(jj * 48, 48), 48), :] = both
            return 0

        lax.fori_loop(0, NFAR // 2, pick_step, 0)
        rows = pl.ds(pl.multiple_of(g * 192, 192), 192)
        combined = nn(coup_v[rows, :], xbuf[...])
        combined = jnp.where(diag, combined, 0.0).astype(BF)
        far = tn(combined, basis_v[rows, :])
        for r in range(8):
            cols = pl.ds(pl.multiple_of((g * 8 + r) * CL, CL), CL)
            val = jbuf[:, cols] + far[r * 16 : r * 16 + 16]
            hi, lo = split(val)
            stack[0:16, cols] = hi
            stack[16:32, cols] = lo
        return 0

    lax.fori_loop(0, NGRP, far_step, 0)

    def inner_step(c, total):
        cols = pl.ds(pl.multiple_of(c * 1024, 1024), 1024)
        s = stack[:, cols]
        return total + nt(s[0:64], s)

    inner = lax.fori_loop(0, ROWS // 1024, inner_step, jnp.zeros((64, 96), F32))
    inner = jnp.concatenate([inner, jnp.zeros((64, 32), F32)], axis=1)
    inner = inner + pltpu.roll(inner, 112, 1)
    j_rows = inner[0:16] + inner[16:32]
    c_rows = pltpu.roll(inner[32:48] + inner[48:64], 16, 1)
    odd = (lane_id // 16) % 2 == 1
    mixed = jnp.where(odd, c_rows, j_rows)

    red_c[core] = mixed
    copy = put(red_c.at[core], red_c.at[core], red_send.at[0], red_recv.at[0], sibling)
    copy.wait_recv()
    mixed = red_c[0] + red_c[1]
    for axis in range(3):
        red_t[axis, pos[axis]] = mixed
        ref = red_t.at[axis, pos[axis]]
        copies = []
        for k, off in enumerate(OFFSETS):
            n = 1 + axis * 3 + k
            copies.append(put(ref, ref, red_send.at[n], red_recv.at[n], shifted(axis, off)))
        for copy in copies:
            copy.wait_recv()
        mixed = (red_t[axis, 0] + red_t[axis, 1]) + (red_t[axis, 2] + red_t[axis, 3])
    mixed = mixed * (1.0 / N)

    jj, cj, jc = mixed[:, 0:16], mixed[:, 16:32], mixed[:, 32:48]
    cc, cv = mixed[:, 48:64], mixed[:, 80:96]
    proj = cj + nt(cv, pc, HIGHEST)
    proj_ref[...] = proj
    a_cj = tn(proj, cj, HIGHEST)
    a_cc = tn(proj, cc, HIGHEST)
    gram = jj - a_cj - nn(jc - a_cc, proj, HIGHEST)

    eye = (lane_id[:, 0:16] == row_id[:, 0:16]).astype(F32)
    m = jnp.concatenate([gram, eye, jnp.zeros((16, 96), F32)], axis=1)
    for k in range(16):
        pivot_row = jnp.broadcast_to(m[k : k + 1, :], (16, 128))
        pivot = m[k : k + 1, k : k + 1]
        factor = jnp.broadcast_to(m[:, k : k + 1] / pivot, (16, 128))
        m = m - jnp.where(row_id > k, factor, 0.0) * pivot_row
    d = jnp.sum(jnp.where(lane_id == row_id, m, 0.0), axis=1, keepdims=True)
    m = m / jnp.sqrt(d)
    upper = jnp.where(lane_id[:, 0:16] >= row_id[:, 0:16], m[:, 0:16], 0.0)
    tri_ref[...] = upper.T
    inverse = m[:, 16:32]
    m2 = -nt(inverse, proj, HIGHEST)
    m1_hi, m1_lo = split(inverse)
    m2_hi, m2_lo = split(m2)
    lhs = jnp.concatenate(
        [
            jnp.concatenate([m1_hi, m1_hi, m2_hi, m2_hi], axis=1),
            jnp.concatenate([m1_lo, m1_lo, m2_lo, m2_lo], axis=1),
        ],
        axis=0,
    )

    def out_step(c, _):
        cols = pl.ds(pl.multiple_of(c * 1024, 1024), 1024)
        both = nn(lhs, stack[0:64, cols])
        out_ref[:, cols] = both[0:16] + both[16:32]
        return 0

    lax.fori_loop(0, ROWS // 1024, out_step, 0)
    for copy in sends:
        copy.wait_send()


def per_device(
    current, previous, prev_coupling, mass_diag, near_blocks, near_cols,
    cluster_basis, coupling, send_list, far_slot,
):
    dma = pltpu.SemaphoreType.DMA
    vmem = pl.BlockSpec(memory_space=pltpu.VMEM)
    hbm = pl.BlockSpec(memory_space=pl.ANY)
    return pl.pallas_call(
        kernel,
        out_shape=(
            jax.ShapeDtypeStruct((NRHS, ROWS), F32),
            jax.ShapeDtypeStruct((NRHS, NRHS), F32),
            jax.ShapeDtypeStruct((NRHS, NRHS), F32),
        ),
        in_specs=[hbm, hbm, vmem, hbm, hbm, vmem, hbm, hbm, vmem, vmem],
        out_specs=(vmem, vmem, vmem),
        scratch_shapes=[
            pltpu.VMEM((NRHS, ROWS), F32),
            pltpu.VMEM((NRHS, ROWS), F32),
            pltpu.VMEM((CPD, CL), F32),
            pltpu.VMEM((CPD * NNEAR, CL, CL), BF),
            pltpu.VMEM((CPD * RANK, CL), BF),
            pltpu.VMEM((CPD * RANK, NFAR * RANK), BF),
            pltpu.VMEM((3 * CPD, NRHS, CL), BF),
            pltpu.VMEM((96, ROWS), BF),
            pltpu.VMEM((NRHS, ROWS), F32),
            pltpu.VMEM((2, 4, 4, 4, PART_ROWS[0], 128), BF),
            pltpu.VMEM((2, 4, 4, 4, PART_ROWS[1], 128), BF),
            pltpu.VMEM((2, 4, 4, 4, PART_ROWS[2], 128), BF),
            pltpu.VMEM((128 * 18, 8, 128), F32),
            pltpu.VMEM((NFAR * RANK, 128), BF),
            pltpu.VMEM((8, 128), jnp.int32),
            pltpu.VMEM((NFAR, 128), jnp.int32),
            pltpu.VMEM((16, 128), jnp.int32),
            pltpu.SMEM((8, 128), jnp.int32),
            pltpu.SMEM((NFAR, 128), jnp.int32),
            pltpu.SMEM((16, 128), jnp.int32),
            pltpu.VMEM((2, 16, 128), F32),
            pltpu.VMEM((3, 4, 16, 128), F32),
            dma((5,)),
            dma((NEAR_CHUNKS,)),
            dma((3,)),
            dma((27,)),
            dma((27,)),
            dma((12,)),
            dma((12,)),
            dma((2,)),
            dma((2,)),
            dma((10,)),
            dma((10,)),
        ],
        compiler_params=pltpu.CompilerParams(
            collective_id=0, has_side_effects=True, vmem_limit_bytes=56 << 20
        ),
    )(
        current,
        previous,
        prev_coupling,
        mass_diag.reshape(CPD, CL),
        near_blocks.reshape(CPD * NNEAR, CL, CL),
        near_cols.T,
        cluster_basis.reshape(CPD * RANK, CL),
        coupling.reshape(CPD * RANK, NFAR * RANK),
        send_list[0].T,
        far_slot.T,
    )


def solution(mesh):
    placed = (
        P(None, ("group", "sub")),
        P(None, ("group", "sub")),
        P(),
        P(("group", "sub")),
        P(("group", "sub"), None, None, None),
        P(("group", "sub"), None),
        P(("group", "sub"), None, None),
        P(("group", "sub"), None, None),
        P(("group", "sub"), None, None),
        P(("group", "sub"), None),
    )
    return jax.shard_map(
        per_device,
        mesh=mesh,
        in_specs=placed,
        out_specs=(P(None, ("group", "sub")), P(), P()),
        check_vma=False,
    )
```

```python
import functools

import jax
import jax.numpy as jnp
from jax import lax
from jax.experimental import pallas as pl
from jax.experimental.pallas import tpu as pltpu
from jax.sharding import PartitionSpec as P

MESH = pl.DeviceIdType.MESH
BF = jnp.bfloat16
F32 = jnp.float32
NRHS = 16
CL = 128
RANK = 24
NNEAR = 8
NFAR = 32
CAP = 12
CPD = 48
NCL = 6144
N = 786432
ROWS = CPD * CL
NGRP = CPD // 8
HIGHEST = lax.Precision.HIGHEST
PART_TILES = (4, 4, 3)
PART_BASE = (0, 512, 1024)
PER_TILE = 5
ORDERS = ((0, 1, 2), (2, 0, 1), (1, 2, 0))
OFFSETS = (2, 1, 3)
NEAR_CHUNKS = 6


def nt(a, b, precision=None):
    return lax.dot_general(
        a, b, (((1,), (1,)), ((), ())), preferred_element_type=F32, precision=precision
    )


def tn(a, b, precision=None):
    return lax.dot_general(
        a, b, (((0,), (0,)), ((), ())), preferred_element_type=F32, precision=precision
    )


def nn(a, b, precision=None):
    return lax.dot_general(
        a, b, (((1,), (0,)), ((), ())), preferred_element_type=F32, precision=precision
    )


def split(x):
    hi = x.astype(BF)
    return hi, (x - hi.astype(F32)).astype(BF)


def kernel(
    cur_h, prev_h, pc_ref, mass_h, near_h, ncol_ref, basis_h, coup_h, slist_ref, far_ref,
    stack, mixed_ref,
    cur_v, prev_v, mass_v, near_v, basis_v, coup_v,
    win, vstack, jbuf, gathered, xbuf,
    ncol_v, far_v, addr_v, ncol_s, far_s, addr_s,
    red_c, red_t,
    load_sem, near_sem, smem_sem,
    ag_send, ag_recv, sib_send, sib_recv, halo_send, halo_recv, red_send, red_recv,
):
    grp = lax.axis_index("group")
    sub = lax.axis_index("sub")
    me = grp * 16 + sub
    core = grp % 2
    pos = (sub % 4, grp // 2, sub // 4)

    def place(x, y, z, c):
        return (y * 2 + c, z * 4 + x)

    def shifted(axis, off):
        at = list(pos)
        at[axis] = (at[axis] + off) % 4
        return place(*at, core)

    sibling = place(*pos, 1 - core)

    def neighbour(off):
        d = (me + off) % 128
        return (d // 16, d % 16)

    loads = []
    for n, (src, dst) in enumerate(
        ((cur_h, cur_v), (basis_h, basis_v), (prev_h, prev_v), (mass_h, mass_v), (coup_h, coup_v))
    ):
        copy = pltpu.make_async_copy(src, dst, load_sem.at[n])
        copy.start()
        loads.append(copy)
    per = CPD * NNEAR // NEAR_CHUNKS
    near_loads = []
    for n in range(NEAR_CHUNKS):
        part = pl.ds(n * per, per)
        copy = pltpu.make_async_copy(near_h.at[part], near_v.at[part], near_sem.at[n])
        copy.start()
        near_loads.append(copy)

    peers = [shifted(a, o) for a in range(3) for o in OFFSETS]
    peers += [sibling, neighbour(1), neighbour(127)]
    barrier = pltpu.get_barrier_semaphore()
    for d in peers:
        pl.semaphore_signal(barrier, inc=1, device_id=d, device_id_type=MESH)

    wanted = ncol_ref[...] - (me - 1) * CPD
    wanted = jnp.where(wanted < 0, wanted + NCL, wanted)
    wanted = jnp.where(wanted >= NCL, wanted - NCL, wanted)
    ncol_v[:, 0:CPD] = jnp.clip(wanted, 0, 3 * CPD - 1)
    q = far_ref[...]
    src = (q * 43691) >> 19
    slot = q - src * CAP
    src_g, src_s = src >> 4, src & 15
    order = (src_g & 1) * 64 + (src_s & 3) * 16 + (src_s >> 2) * 4 + (src_g >> 1)
    far_v[:, 0:CPD] = jnp.clip(order * 16 + slot, 0, 2047)
    ncol_copy = pltpu.make_async_copy(ncol_v, ncol_s, smem_sem.at[0])
    far_copy = pltpu.make_async_copy(far_v, far_s, smem_sem.at[1])
    ncol_copy.start()
    far_copy.start()

    loads[0].wait()

    def window_step(c, _):
        cols = pl.ds(pl.multiple_of(c * CL, CL), CL)
        hi, lo = split(cur_v[:, cols])
        win[CPD + c] = hi
        stack[32:48, cols] = hi
        stack[48:64, cols] = lo
        return 0

    lax.fori_loop(0, CPD, window_step, 0, unroll=4)
    pl.semaphore_wait(barrier, len(peers))

    sends = []

    def put(src_ref, dst_ref, send_sem, recv_sem, device):
        copy = pltpu.make_async_remote_copy(
            src_ref=src_ref, dst_ref=dst_ref, send_sem=send_sem, recv_sem=recv_sem,
            device_id=device, device_id_type=MESH,
        )
        copy.start()
        sends.append(copy)
        return copy

    mid = win.at[pl.ds(CPD, CPD)]
    halo = [
        put(mid, win.at[pl.ds(0, CPD)], halo_send.at[0], halo_recv.at[0], neighbour(1)),
        put(mid, win.at[pl.ds(2 * CPD, CPD)], halo_send.at[1], halo_recv.at[1], neighbour(127)),
    ]

    loads[1].wait()
    tiles = []
    for m in range(10):
        count = min(PER_TILE, CPD - m * PER_TILE)
        cl = win[CPD + m * PER_TILE : CPD + m * PER_TILE + count].reshape(count * NRHS, CL)
        y = nt(cl, basis_v[m * PER_TILE * RANK : (m * PER_TILE + count) * RANK, :])
        shape = (count * NRHS, count * RANK)
        diag = lax.broadcasted_iota(jnp.int32, shape, 0) // NRHS == (
            lax.broadcasted_iota(jnp.int32, shape, 1) // RANK
        )
        y = jnp.sum(jnp.where(diag, y, 0.0).reshape(count, NRHS, count * RANK), axis=0)
        y = jnp.concatenate([y, jnp.zeros((NRHS, 128 - count * RANK), F32)], axis=1)
        tiles.append(y.astype(BF))
    slist = jnp.concatenate([slist_ref[...].reshape(CAP, 128).astype(F32), jnp.zeros((4, 128), F32)], axis=0)
    tiles.append(slist.astype(BF))

    def block(p, phase, off):
        at = [pos[a] for a in ORDERS[p]]
        at[phase] = (at[phase] + off) % 4
        size = PART_TILES[p]
        first = ((core * 4 + at[2]) * 4 + at[1]) * 4 + at[0]
        if phase == 1:
            first, size = (core * 4 + at[2]) * 4 + at[1], size * 4
        elif phase == 2:
            first, size = core * 4 + at[2], size * 16
        return gathered.at[pl.ds(PART_BASE[p] + first * size, size)]

    done = 0
    for p in range(3):
        own = block(p, 0, 0)
        for i in range(PART_TILES[p]):
            own[i] = tiles[done + i]
        done += PART_TILES[p]

    def gather_phase(phase):
        copies = []
        for k, off in enumerate(OFFSETS):
            for p in range(3):
                n = (phase * 3 + p) * 3 + k
                ref = block(p, phase, 0)
                copies.append(
                    put(ref, ref, ag_send.at[n], ag_recv.at[n], shifted(ORDERS[p][phase], off))
                )
        return copies

    sib_copies = []

    def to_sibling(ref):
        n = len(sib_copies)
        sib_copies.append(put(ref, ref, sib_send.at[n], sib_recv.at[n], sibling))

    phase1 = gather_phase(0)
    loads[2].wait()
    pc = pc_ref[...]
    pc_hi, pc_lo = split(pc)
    pc_rows = jnp.concatenate([pc_hi, pc_hi], axis=1)
    pc_rows2 = jnp.concatenate([pc_lo, pc_lo], axis=1)
    pc_all = jnp.concatenate([pc_rows, pc_rows2], axis=0)

    def previous_step(c, _):
        cols = pl.ds(pl.multiple_of(c * 512, 512), 512)
        hi, lo = split(prev_v[:, cols])
        vstack[0:16, cols] = hi
        vstack[16:32, cols] = lo
        both = nn(pc_all, jnp.concatenate([hi, lo], axis=0))
        jbuf[:, cols] = -(both[0:16] + both[16:32])
        return 0

    lax.fori_loop(0, ROWS // 512, previous_step, 0)

    for copy in phase1:
        copy.wait_recv()
    phase2 = gather_phase(1)
    loads[3].wait()
    loads[4].wait()
    for copy in phase2:
        copy.wait_recv()
    phase3 = gather_phase(2)
    for p in range(3):
        to_sibling(block(p, 2, 0))

    ncol_copy.wait()
    for copy in halo:
        copy.wait_recv()

    def near_step(r, _):
        xs, ms = [], []
        for j in range(NNEAR):
            w = ncol_s[j, r]
            xs.append(win[w])
        x = jnp.concatenate(xs, axis=1)
        m = near_v[pl.ds(r * NNEAR, NNEAR)]
        m = jnp.concatenate([m[j] for j in range(NNEAR)], axis=1)
        cols = pl.ds(pl.multiple_of(r * CL, CL), CL)
        jbuf[:, cols] += nt(x, m) + mass_v[pl.ds(r, 1), :] * cur_v[:, cols]
        return 0

    rows_per = CPD // NEAR_CHUNKS
    for n in range(NEAR_CHUNKS):
        near_loads[n].wait()
        lax.fori_loop(n * rows_per, (n + 1) * rows_per, near_step, 0)

    for copy in phase3:
        copy.wait_recv()
    for p in range(3):
        for off in (1, 2, 3):
            to_sibling(block(p, 2, off))
    far_copy.wait()
    for copy in sib_copies:
        copy.wait_recv()

    lists = gathered[PART_BASE[2] : PART_BASE[2] + 384].reshape(128, 3, 16, 128)[:, 2]
    mine = (lax.broadcasted_iota(jnp.int32, (16, 128), 1) == me).astype(BF)
    local = nt(mine, lists.reshape(2048, 128))[0:1]
    local = jnp.clip(local.astype(jnp.int32), 0, CPD - 1)
    t = lax.broadcasted_iota(jnp.int32, (1, 2048), 1) >> 4
    sy, sz, sx, sc = t & 3, (t >> 2) & 3, (t >> 4) & 3, t >> 6
    tile = (local * 13) >> 6
    at_a = (((sc * 4 + sz) * 4 + sy) * 4 + sx) * 4 + tile
    at_b = PART_BASE[1] + (((sc * 4 + sy) * 4 + sx) * 4 + sz) * 4 + tile - 4
    at_c = PART_BASE[2] + t * 3 + tile - 8
    at = jnp.where(tile < 4, at_a, jnp.where(tile < 8, at_b, at_c))
    turn = (128 - (local - tile * PER_TILE) * RANK) & 127
    addr_v[...] = jnp.clip(at, 0, 1407) * 128 + turn
    addr_copy = pltpu.make_async_copy(addr_v, addr_s, smem_sem.at[2])
    addr_copy.start()
    addr_copy.wait()

    lane = lax.broadcasted_iota(jnp.int32, (16, 128), 1)
    diag = lax.broadcasted_iota(jnp.int32, (128, 8 * RANK), 0) // NRHS == (
        lax.broadcasted_iota(jnp.int32, (128, 8 * RANK), 1) // RANK
    )

    def far_step(g, _):
        def pick_step(r, _):
            total = [None] * 6
            for j in range(NFAR):
                word = addr_s[0, far_s[j, g * 8 + r]]
                rows = pltpu.roll(gathered[word >> 7], (word + j * RANK) & 127, 1)
                k, first = j * RANK // 128, j * RANK % 128
                total[k] = rows if first == 0 else jnp.where(lane >= first, rows, total[k])
                if first + RANK > 128:
                    total[k + 1] = rows
            xbuf[pl.ds(pl.multiple_of(r * 16, 16), 16), :] = jnp.concatenate(total, axis=1)
            return 0

        lax.fori_loop(0, 8, pick_step, 0)
        rows = pl.ds(pl.multiple_of(g * 192, 192), 192)
        combined = nt(xbuf[...], coup_v[rows, :])
        combined = jnp.where(diag, combined, 0.0).astype(BF)
        far = nn(combined, basis_v[rows, :])
        for r in range(8):
            cols = pl.ds(pl.multiple_of((g * 8 + r) * CL, CL), CL)
            val = jbuf[:, cols] + far[r * 16 : r * 16 + 16]
            hi, lo = split(val)
            stack[0:16, cols] = hi
            stack[16:32, cols] = lo
        return 0

    lax.fori_loop(0, NGRP, far_step, 0)

    def inner_step(c, total):
        cols = pl.ds(pl.multiple_of(c * 1024, 1024), 1024)
        s = stack[:, cols]
        return total + nt(s, jnp.concatenate([s, vstack[:, cols]], axis=0))

    inner = lax.fori_loop(0, ROWS // 1024, inner_step, jnp.zeros((64, 96), F32))
    inner = jnp.concatenate([inner, jnp.zeros((64, 32), F32)], axis=1)
    inner = inner + pltpu.roll(inner, 112, 1)
    j_rows = inner[0:16] + inner[16:32]
    c_rows = pltpu.roll(inner[32:48] + inner[48:64], 16, 1)
    odd = (lane // 16) % 2 == 1
    mixed = jnp.where(odd, c_rows, j_rows)

    red_c[core] = mixed
    copy = put(red_c.at[core], red_c.at[core], red_send.at[0], red_recv.at[0], sibling)
    copy.wait_recv()
    mixed = red_c[0] + red_c[1]
    for axis in range(3):
        red_t[axis, pos[axis]] = mixed
        ref = red_t.at[axis, pos[axis]]
        copies = []
        for k, off in enumerate(OFFSETS):
            n = 1 + axis * 3 + k
            copies.append(put(ref, ref, red_send.at[n], red_recv.at[n], shifted(axis, off)))
        for copy in copies:
            copy.wait_recv()
        mixed = (red_t[axis, 0] + red_t[axis, 1]) + (red_t[axis, 2] + red_t[axis, 3])
    mixed_ref[...] = mixed * (1.0 / N)
    for copy in sends:
        copy.wait_send()


def finish(stack, mixed_ref, pc_ref, out_ref, proj_ref, tri_ref):
    mixed = mixed_ref[...]
    pc = pc_ref[...]
    row_id = lax.broadcasted_iota(jnp.int32, (16, 128), 0)
    lane_id = lax.broadcasted_iota(jnp.int32, (16, 128), 1)
    jj, cj, jc = mixed[:, 0:16], mixed[:, 16:32], mixed[:, 32:48]
    cc, cv = mixed[:, 48:64], mixed[:, 80:96]
    proj = cj + nt(cv, pc, HIGHEST)
    proj_ref[...] = proj
    a_cj = tn(proj, cj, HIGHEST)
    a_cc = tn(proj, cc, HIGHEST)
    gram = jj - a_cj - nn(jc - a_cc, proj, HIGHEST)

    eye = (lane_id[:, 0:16] == row_id[:, 0:16]).astype(F32)
    m = jnp.concatenate([gram, eye, jnp.zeros((16, 96), F32)], axis=1)
    for k in range(16):
        pivot_row = jnp.broadcast_to(m[k : k + 1, :], (16, 128))
        pivot = m[k : k + 1, k : k + 1]
        factor = jnp.broadcast_to(m[:, k : k + 1] / pivot, (16, 128))
        m = m - jnp.where(row_id > k, factor, 0.0) * pivot_row
    d = jnp.sum(jnp.where(lane_id == row_id, m, 0.0), axis=1, keepdims=True)
    m = m / jnp.sqrt(d)
    upper = jnp.where(lane_id[:, 0:16] >= row_id[:, 0:16], m[:, 0:16], 0.0)
    tri_ref[...] = upper.T
    inverse = m[:, 16:32]
    m2 = -nt(inverse, proj, HIGHEST)
    m1_hi, m1_lo = split(inverse)
    m2_hi, m2_lo = split(m2)
    lhs = jnp.concatenate(
        [
            jnp.concatenate([m1_hi, m1_hi, m2_hi, m2_hi], axis=1),
            jnp.concatenate([m1_lo, m1_lo, m2_lo, m2_lo], axis=1),
        ],
        axis=0,
    )

    def out_step(c, _):
        cols = pl.ds(pl.multiple_of(c * 1024, 1024), 1024)
        both = nn(lhs, stack[:, cols])
        out_ref[:, cols] = both[0:16] + both[16:32]
        return 0

    lax.fori_loop(0, ROWS // 1024, out_step, 0)


def per_device(
    current, previous, prev_coupling, mass_diag, near_blocks, near_cols,
    cluster_basis, coupling, send_list, far_slot,
):
    dma = pltpu.SemaphoreType.DMA
    vmem = pl.BlockSpec(memory_space=pltpu.VMEM)
    hbm = pl.BlockSpec(memory_space=pl.ANY)
    stack, mixed = pl.pallas_call(
        kernel,
        out_shape=(
            jax.ShapeDtypeStruct((64, ROWS), BF),
            jax.ShapeDtypeStruct((NRHS, 128), F32),
        ),
        in_specs=[hbm, hbm, vmem, hbm, hbm, vmem, hbm, hbm, vmem, vmem],
        out_specs=(vmem, vmem),
        scratch_shapes=[
            pltpu.VMEM((NRHS, ROWS), F32),
            pltpu.VMEM((NRHS, ROWS), F32),
            pltpu.VMEM((CPD, CL), F32),
            pltpu.VMEM((CPD * NNEAR, CL, CL), BF),
            pltpu.VMEM((CPD * RANK, CL), BF),
            pltpu.VMEM((CPD * RANK, NFAR * RANK), BF),
            pltpu.VMEM((3 * CPD, NRHS, CL), BF),
            pltpu.VMEM((32, ROWS), BF),
            pltpu.VMEM((NRHS, ROWS), F32),
            pltpu.VMEM((128 * 11, NRHS, 128), BF),
            pltpu.VMEM((128, NFAR * RANK), BF),
            pltpu.VMEM((8, 128), jnp.int32),
            pltpu.VMEM((NFAR, 128), jnp.int32),
            pltpu.VMEM((1, 2048), jnp.int32),
            pltpu.SMEM((8, 128), jnp.int32),
            pltpu.SMEM((NFAR, 128), jnp.int32),
            pltpu.SMEM((1, 2048), jnp.int32),
            pltpu.VMEM((2, 16, 128), F32),
            pltpu.VMEM((3, 4, 16, 128), F32),
            dma((5,)),
            dma((NEAR_CHUNKS,)),
            dma((3,)),
            dma((27,)),
            dma((27,)),
            dma((12,)),
            dma((12,)),
            dma((2,)),
            dma((2,)),
            dma((10,)),
            dma((10,)),
        ],
        compiler_params=pltpu.CompilerParams(
            collective_id=0, has_side_effects=True, vmem_limit_bytes=56 << 20
        ),
    )(
        current,
        previous,
        prev_coupling,
        mass_diag.reshape(CPD, CL),
        near_blocks.reshape(CPD * NNEAR, CL, CL),
        near_cols.T,
        cluster_basis.reshape(CPD * RANK, CL),
        coupling.reshape(CPD * RANK, NFAR * RANK),
        send_list.transpose(2, 0, 1),
        far_slot.T,
    )
    return pl.pallas_call(
        finish,
        out_shape=(
            jax.ShapeDtypeStruct((NRHS, ROWS), F32),
            jax.ShapeDtypeStruct((NRHS, NRHS), F32),
            jax.ShapeDtypeStruct((NRHS, NRHS), F32),
        ),
        in_specs=[vmem, vmem, vmem],
        out_specs=(vmem, vmem, vmem),
    )(stack, mixed, prev_coupling)


def solution(mesh):
    placed = (
        P(None, ("group", "sub")),
        P(None, ("group", "sub")),
        P(),
        P(("group", "sub")),
        P(("group", "sub"), None, None, None),
        P(("group", "sub"), None),
        P(("group", "sub"), None, None),
        P(("group", "sub"), None, None),
        P(("group", "sub"), None, None),
        P(("group", "sub"), None),
    )
    return jax.shard_map(
        per_device,
        mesh=mesh,
        in_specs=placed,
        out_specs=(P(None, ("group", "sub")), P(), P()),
        check_vma=False,
    )
```

```python
import functools

import jax
import jax.numpy as jnp
from jax import lax
from jax.experimental import pallas as pl
from jax.experimental.pallas import tpu as pltpu
from jax.sharding import PartitionSpec as P

MESH = pl.DeviceIdType.MESH
BF = jnp.bfloat16
F32 = jnp.float32
NRHS = 16
CL = 128
RANK = 24
NNEAR = 8
NFAR = 32
CAP = 12
CPD = 48
NCL = 6144
N = 786432
ROWS = CPD * CL
NGRP = CPD // 8
HIGHEST = lax.Precision.HIGHEST
PART_TILES = (4, 4, 2)
PART_BASE = (0, 512, 1024)
PER_TILE = 5
ORDERS = ((0, 1, 2), (2, 0, 1), (1, 2, 0))
OFFSETS = (2, 1, 3)
VIA_UP = (0, 1)
XC = [(dx, dc) for dx in range(4) for dc in range(2) if dx or dc]
YZ = [(dy, dz) for dy in range(4) for dz in range(4) if dy or dz]
TILES = 1280
NEAR_CHUNKS = 6


def nt(a, b, precision=None):
    return lax.dot_general(
        a, b, (((1,), (1,)), ((), ())), preferred_element_type=F32, precision=precision
    )


def tn(a, b, precision=None):
    return lax.dot_general(
        a, b, (((0,), (0,)), ((), ())), preferred_element_type=F32, precision=precision
    )


def nn(a, b, precision=None):
    return lax.dot_general(
        a, b, (((1,), (0,)), ((), ())), preferred_element_type=F32, precision=precision
    )


def split(x):
    hi = x.astype(BF)
    return hi, (x - hi.astype(F32)).astype(BF)


def kernel(
    cur_h, prev_h, pc_h, mass_h, near_h, ncol_h, basis_h, coup_h, slist_h, far_h,
    stack_h, mixed_ref,
    cur_v, prev_v, pc_v, mass_v, near_v, basis_v, coup_v, slist_v, ncol_v, far_v,
    win, stack, vbuf, ibuf, gathered, lists, xbuf,
    addr_v, ncol_s, far_s, addr_s,
    red_a, red_b,
    load_sem, near_sem, smem_sem, out_sem,
    p1_send, p1_recv, p2_send, p2_recv, p3_send, p3_recv, list_send, list_recv,
    sib_send, sib_recv, halo_send, halo_recv, red_send, red_recv,
):
    grp = lax.axis_index("group")
    sub = lax.axis_index("sub")
    me = grp * 16 + sub
    core = grp % 2
    pos = (sub % 4, grp // 2, sub // 4)

    def place(x, y, z, c):
        return (y * 2 + c, z * 4 + x)

    def shifted(axis, off):
        at = list(pos)
        at[axis] = (at[axis] + off) % 4
        return place(*at, core)

    def at_xc(dx, dc):
        return place((pos[0] + dx) % 4, pos[1], pos[2], (core + dc) % 2)

    def at_yz(dy, dz):
        return place(pos[0], (pos[1] + dy) % 4, (pos[2] + dz) % 4, core)

    sibling = place(*pos, 1 - core)

    def neighbour(off):
        d = (me + off) % 128
        return (d // 16, d % 16)

    loads = {}
    for n, (name, src, dst) in enumerate(
        (
            ("cur", cur_h, cur_v), ("basis", basis_h, basis_v), ("slist", slist_h, slist_v),
            ("ncol", ncol_h, ncol_v), ("far", far_h, far_v), ("pc", pc_h, pc_v),
            ("prev", prev_h, prev_v), ("mass", mass_h, mass_v), ("coup", coup_h, coup_v),
        )
    ):
        loads[name] = pltpu.make_async_copy(src, dst, load_sem.at[n])
        loads[name].start()
    per = CPD * NNEAR // NEAR_CHUNKS
    near_loads = []
    for n in range(NEAR_CHUNKS):
        part = pl.ds(n * per, per)
        copy = pltpu.make_async_copy(near_h.at[part], near_v.at[part], near_sem.at[n])
        copy.start()
        near_loads.append(copy)

    peers = [at_xc(dx, dc) for dx, dc in XC] + [at_yz(dy, dz) for dy, dz in YZ]
    peers += [neighbour(1), neighbour(127)]
    barrier = pltpu.get_barrier_semaphore()
    for d in peers:
        pl.semaphore_signal(barrier, inc=1, device_id=d, device_id_type=MESH)

    loads["cur"].wait()

    def window_step(c, _):
        cols = pl.ds(pl.multiple_of(c * CL, CL), CL)
        hi, lo = split(cur_v[:, cols])
        win[CPD + c] = hi
        stack[32:48, cols] = hi
        stack[48:64, cols] = lo
        return 0

    lax.fori_loop(0, CPD, window_step, 0, unroll=4)
    pl.semaphore_wait(barrier, len(peers))

    sends = []

    def put(src_ref, dst_ref, send_sem, recv_sem, device):
        copy = pltpu.make_async_remote_copy(
            src_ref=src_ref, dst_ref=dst_ref, send_sem=send_sem, recv_sem=recv_sem,
            device_id=device, device_id_type=MESH,
        )
        copy.start()
        sends.append(copy)
        return copy

    mid = win.at[pl.ds(CPD, CPD)]
    halo = [
        put(mid, win.at[pl.ds(0, CPD)], halo_send.at[0], halo_recv.at[0], neighbour(1)),
        put(mid, win.at[pl.ds(2 * CPD, CPD)], halo_send.at[1], halo_recv.at[1], neighbour(127)),
    ]

    loads["basis"].wait()
    tiles = []
    for m in range(10):
        count = min(PER_TILE, CPD - m * PER_TILE)
        cl = win[CPD + m * PER_TILE : CPD + m * PER_TILE + count].reshape(count * NRHS, CL)
        y = nt(cl, basis_v[m * PER_TILE * RANK : (m * PER_TILE + count) * RANK, :])
        shape = (count * NRHS, count * RANK)
        diag = lax.broadcasted_iota(jnp.int32, shape, 0) // NRHS == (
            lax.broadcasted_iota(jnp.int32, shape, 1) // RANK
        )
        y = jnp.sum(jnp.where(diag, y, 0.0).reshape(count, NRHS, count * RANK), axis=0)
        y = jnp.concatenate([y, jnp.zeros((NRHS, 128 - count * RANK), F32)], axis=1)
        tiles.append(y.astype(BF))
    loads["slist"].wait()
    slist = slist_v[...].reshape(CAP, 128).astype(F32)
    slist = jnp.concatenate([slist, jnp.zeros((4, 128), F32)], axis=0).astype(BF)

    def chunk(p):
        at = [pos[a] for a in ORDERS[p]]
        first = ((core * 4 + at[2]) * 4 + at[1]) * 4 + at[0]
        return gathered.at[pl.ds(PART_BASE[p] + first * PART_TILES[p], PART_TILES[p])]

    def rows_of(p, k2, k3):
        at = [pos[a] for a in ORDERS[p]]
        first = (core * 4 + (at[2] + k3) % 4) * 4 + (at[1] + k2) % 4
        size = 4 * PART_TILES[p]
        return gathered.at[pl.ds(PART_BASE[p] + first * size, size)]

    def plane_of(p):
        size = 16 * PART_TILES[p]
        return gathered.at[pl.ds(PART_BASE[p] + (core * 4 + pos[ORDERS[p][2]]) * size, size)]

    def list_block(phase):
        first = core * 64 + pos[2] * 16
        if phase < 2:
            first = first + pos[1] * 4
        if phase < 1:
            first = first + pos[0]
        return lists.at[pl.ds(first, 4**phase)]

    done = 0
    for p in range(3):
        own = chunk(p)
        for i in range(PART_TILES[p]):
            own[i] = tiles[done + i]
        done += PART_TILES[p]
    list_block(0)[0] = slist

    def spread(ref, axis, sems, n):
        return {
            off: put(ref, ref, sems[0].at[n + k], sems[1].at[n + k], shifted(axis, off))
            for k, off in enumerate(OFFSETS)
        }

    def spread_list(phase):
        return spread(list_block(phase), phase, (list_send, list_recv), 3 * phase)

    def arrive(copies):
        for copy in copies.values():
            copy.wait_recv()

    sib_copies = []

    def to_sibling(ref):
        n = len(sib_copies)
        sib_copies.append(put(ref, ref, sib_send.at[n], sib_recv.at[n], sibling))

    phase3 = {}

    def start3(p, k2):
        axis = ORDERS[p][2]
        ref = rows_of(p, k2, 0)
        n = (p * 4 + k2) * 3
        phase3[p, k2] = [
            put(ref, ref, p3_send.at[n], p3_recv.at[n], shifted(axis, 1)),
            put(ref, ref, p3_send.at[n + 1], p3_recv.at[n + 1], shifted(axis, 3)),
        ]

    def relay3(k2):
        for p in range(3):
            axis = ORDERS[p][2]
            n = (p * 4 + k2) * 3 + 2
            up = k2 in VIA_UP
            phase3[p, k2][0 if up else 1].wait_recv()
            ref = rows_of(p, k2, 3 if up else 1)
            phase3[p, k2].append(
                put(ref, ref, p3_send.at[n], p3_recv.at[n], shifted(axis, 1 if up else 3))
            )
        for p in range(3):
            phase3[p, k2][1 if k2 in VIA_UP else 0].wait_recv()

    phase1 = [spread(chunk(p), ORDERS[p][0], (p1_send, p1_recv), 3 * p) for p in range(3)]
    lists1 = spread_list(0)

    loads["ncol"].wait()
    wanted = ncol_v[...] - (me - 1) * CPD
    wanted = jnp.where(wanted < 0, wanted + NCL, wanted)
    wanted = jnp.where(wanted >= NCL, wanted - NCL, wanted)
    ncol_v[...] = jnp.clip(wanted, 0, 3 * CPD - 1)
    loads["far"].wait()
    q = far_v[...]
    src = (q * 43691) >> 19
    slot = q - src * CAP
    src_g, src_s = src >> 4, src & 15
    order = (src_g & 1) * 64 + (src_s >> 2) * 16 + (src_g >> 1) * 4 + (src_s & 3)
    far_v[...] = jnp.clip(order * 16 + slot, 0, 2047)
    ncol_copy = pltpu.make_async_copy(ncol_v, ncol_s, smem_sem.at[0])
    far_copy = pltpu.make_async_copy(far_v, far_s, smem_sem.at[1])
    ncol_copy.start()
    far_copy.start()

    loads["pc"].wait()
    loads["prev"].wait()
    pc = pc_v[...]
    pc_hi, pc_lo = split(pc)
    pc_rows = jnp.concatenate([pc_hi, pc_hi], axis=1)
    pc_rows2 = jnp.concatenate([pc_lo, pc_lo], axis=1)
    pc_all = jnp.concatenate([pc_rows, pc_rows2], axis=0)

    def previous_step(c, _):
        cols = pl.ds(pl.multiple_of(c * 512, 512), 512)
        hi, lo = split(prev_v[:, cols])
        both = nn(pc_all, jnp.concatenate([hi, lo], axis=0))
        vbuf[:, cols] = both[0:16] + both[16:32]
        return 0

    lax.fori_loop(0, ROWS // 512, previous_step, 0)

    for copies in phase1:
        arrive(copies)
    arrive(lists1)
    lists2 = spread_list(1)
    phase2 = [spread(rows_of(p, 0, 0), ORDERS[p][1], (p2_send, p2_recv), 3 * p) for p in range(3)]
    for p in range(3):
        start3(p, 0)
    loads["mass"].wait()
    loads["coup"].wait()
    ncol_copy.wait()
    far_copy.wait()
    arrive(lists2)
    lists3 = spread_list(2)
    for k2, off in ((1, 3), (3, 1), (2, 2)):
        if k2 == 2:
            relay3(0)
        for p in range(3):
            phase2[p][off].wait_recv()
            start3(p, k2)
    for p in range(3):
        to_sibling(plane_of(p))

    for copy in halo:
        copy.wait_recv()

    def near_step(r, _):
        xs, ms = [], []
        for j in range(NNEAR):
            w = ncol_s[j, r]
            xs.append(win[w])
        x = jnp.concatenate(xs, axis=1)
        m = near_v[pl.ds(r * NNEAR, NNEAR)]
        m = jnp.concatenate([m[j] for j in range(NNEAR)], axis=1)
        cols = pl.ds(pl.multiple_of(r * CL, CL), CL)
        ibuf[:, cols] = nt(x, m) + mass_v[pl.ds(r, 1), :] * cur_v[:, cols]
        return 0

    def near_chunk(n):
        rows_per = CPD // NEAR_CHUNKS
        near_loads[n].wait()
        lax.fori_loop(n * rows_per, (n + 1) * rows_per, near_step, 0, unroll=4)

    def forward3(k2):
        for p in range(3):
            to_sibling(rows_of(p, k2, 1))
            to_sibling(rows_of(p, k2, 3))

    near_chunk(0)
    arrive(lists3)
    list_plane = lists.at[pl.ds(core * 64, 64)]
    list_sib = put(list_plane, list_plane, list_send.at[9], list_recv.at[9], sibling)
    near_chunk(1)
    relay3(1)
    forward3(0)
    forward3(1)
    near_chunk(2)
    near_chunk(3)
    relay3(3)
    forward3(3)
    near_chunk(4)
    list_sib.wait_recv()

    mine = (lax.broadcasted_iota(jnp.int32, (16, 128), 1) == me).astype(BF)
    local = nt(mine, lists[...].reshape(2048, 128))[0:1]
    local = jnp.clip(local.astype(jnp.int32), 0, CPD - 1)
    t = lax.broadcasted_iota(jnp.int32, (1, 2048), 1) >> 4
    sx, sy, sz, sc = t & 3, (t >> 2) & 3, (t >> 4) & 3, t >> 6
    tile = (local * 13) >> 6
    at_a = (((sc * 4 + sz) * 4 + sy) * 4 + sx) * 4 + tile
    at_b = PART_BASE[1] + (((sc * 4 + sy) * 4 + sx) * 4 + sz) * 4 + tile - 4
    at_c = PART_BASE[2] + (((sc * 4 + sx) * 4 + sz) * 4 + sy) * 2 + tile - 8
    at = jnp.where(tile < 4, at_a, jnp.where(tile < 8, at_b, at_c))
    turn = (128 - (local - tile * PER_TILE) * RANK) & 127
    addr_v[...] = jnp.clip(at, 0, TILES - 1) * 128 + turn
    addr_copy = pltpu.make_async_copy(addr_v, addr_s, smem_sem.at[2])
    addr_copy.start()
    near_chunk(5)
    relay3(2)
    forward3(2)
    for k2 in (0, 1, 3, 2):
        for p in range(3):
            phase3[p, k2][2].wait_recv()
            to_sibling(rows_of(p, k2, 2))
    addr_copy.wait()
    for copy in sib_copies:
        copy.wait_recv()

    lane = lax.broadcasted_iota(jnp.int32, (16, 128), 1)
    diag = lax.broadcasted_iota(jnp.int32, (128, 8 * RANK), 0) // NRHS == (
        lax.broadcasted_iota(jnp.int32, (128, 8 * RANK), 1) // RANK
    )

    def far_step(g, total_inner):
        def pick_step(r, _):
            total = [None] * 6
            for j in range(NFAR):
                word = addr_s[0, far_s[j, g * 8 + r]]
                rows = pltpu.roll(gathered[word >> 7], (word + j * RANK) & 127, 1)
                k, first = j * RANK // 128, j * RANK % 128
                total[k] = rows if first == 0 else jnp.where(lane >= first, rows, total[k])
                if first + RANK > 128:
                    total[k + 1] = rows
            xbuf[pl.ds(pl.multiple_of(r * 16, 16), 16), :] = jnp.concatenate(total, axis=1)
            return 0

        lax.fori_loop(0, 8, pick_step, 0, unroll=8)
        rows = pl.ds(pl.multiple_of(g * 192, 192), 192)
        combined = nt(xbuf[...], coup_v[rows, :])
        combined = jnp.where(diag, combined, 0.0).astype(BF)
        far = nn(combined, basis_v[rows, :])
        cols = pl.ds(pl.multiple_of(g * 1024, 1024), 1024)
        far = jnp.concatenate([far[r * 16 : r * 16 + 16] for r in range(8)], axis=1)
        image = ibuf[:, cols] + far
        j_hi, j_lo = split(image - vbuf[:, cols])
        i_hi, i_lo = split(image)
        stack[0:16, cols] = j_hi
        stack[16:32, cols] = j_lo
        s = jnp.concatenate([j_hi, j_lo, stack[32:64, cols]], axis=0)
        return total_inner + nt(s, jnp.concatenate([s, i_hi, i_lo], axis=0))

    inner = lax.fori_loop(0, NGRP, far_step, jnp.zeros((64, 96), F32))
    stack_copy = pltpu.make_async_copy(stack, stack_h, out_sem)
    stack_copy.start()

    inner = jnp.concatenate([inner, jnp.zeros((64, 32), F32)], axis=1)
    inner = inner + pltpu.roll(inner, 112, 1)
    j_rows = inner[0:16] + inner[16:32]
    c_rows = inner[32:48] + inner[48:64]
    mixed = jnp.where(lane < 48, c_rows, pltpu.roll(c_rows, 112, 1))
    mixed = jnp.where(lane < 32, pltpu.roll(c_rows, 16, 1), mixed)
    mixed = jnp.where(lane < 16, j_rows, mixed)
    mixed = jnp.where(lane[0:8] < 64, mixed[0:8], pltpu.roll(mixed[8:16], 64, 1))

    def reduce(value, buf, place_at, devices, n):
        buf[place_at] = value
        ref = buf.at[place_at]
        copies = [
            put(ref, ref, red_send.at[n + k], red_recv.at[n + k], d) for k, d in enumerate(devices)
        ]
        for copy in copies:
            copy.wait_recv()
        parts = [buf[k] for k in range(len(devices) + 1)]
        while len(parts) > 1:
            parts = [a + b for a, b in zip(parts[::2], parts[1::2])]
        return parts[0]

    mixed = reduce(mixed, red_a, pos[0] * 2 + core, [at_xc(*o) for o in XC], 0)
    mixed = reduce(mixed, red_b, pos[1] * 4 + pos[2], [at_yz(*o) for o in YZ], 7)
    mixed_ref[...] = mixed * (1.0 / N)
    stack_copy.wait()
    for copy in sends:
        copy.wait_send()


def finish(stack_h, mixed_ref, out_h, proj_ref, tri_ref, stack, out_v, load_sem, out_sem):
    half = ROWS // 2
    loads = []
    for n in range(2):
        part = pl.ds(n * half, half)
        loads.append(
            pltpu.make_async_copy(stack_h.at[:, part], stack.at[:, part], load_sem.at[n])
        )
        loads[n].start()
    mixed = mixed_ref[...]
    mixed = jnp.concatenate([mixed, pltpu.roll(mixed, 64, 1)], axis=0)
    row_id = lax.broadcasted_iota(jnp.int32, (16, 128), 0)
    lane_id = lax.broadcasted_iota(jnp.int32, (16, 128), 1)
    jj, cj, cc, proj = mixed[:, 0:16], mixed[:, 16:32], mixed[:, 32:48], mixed[:, 48:64]
    proj_ref[...] = proj
    both = tn(proj, mixed[:, 16:48], HIGHEST)
    gram = jj - both[:, 0:16] - nn(cj.T - both[:, 16:32], proj, HIGHEST)

    eye = (lane_id[:, 0:16] == row_id[:, 0:16]).astype(F32)
    m = jnp.concatenate([gram, eye, jnp.zeros((16, 96), F32)], axis=1)
    for k in range(16):
        pivot_row = jnp.broadcast_to(m[k : k + 1, :], (16, 128))
        pivot = m[k : k + 1, k : k + 1]
        factor = jnp.broadcast_to(m[:, k : k + 1] / pivot, (16, 128))
        m = m - jnp.where(row_id > k, factor, 0.0) * pivot_row
    d = jnp.sum(jnp.where(lane_id == row_id, m, 0.0), axis=1, keepdims=True)
    m = m / jnp.sqrt(d)
    upper = jnp.where(lane_id[:, 0:16] >= row_id[:, 0:16], m[:, 0:16], 0.0)
    tri_ref[...] = upper.T
    inverse = m[:, 16:32]
    m2 = -nt(inverse, proj, HIGHEST)
    m1_hi, m1_lo = split(inverse)
    m2_hi, m2_lo = split(m2)
    lhs = jnp.concatenate(
        [
            jnp.concatenate([m1_hi, m1_hi, m2_hi, m2_hi], axis=1),
            jnp.concatenate([m1_lo, m1_lo, m2_lo, m2_lo], axis=1),
        ],
        axis=0,
    )

    def out_step(c, _):
        cols = pl.ds(pl.multiple_of(c * 1024, 1024), 1024)
        both = nn(lhs, stack[:, cols])
        out_v[:, cols] = both[0:16] + both[16:32]
        return 0

    stores = []
    for n in range(2):
        part = pl.ds(n * half, half)
        loads[n].wait()
        lax.fori_loop(n * 3, n * 3 + 3, out_step, 0, unroll=3)
        stores.append(pltpu.make_async_copy(out_v.at[:, part], out_h.at[:, part], out_sem.at[n]))
        stores[n].start()
    for copy in stores:
        copy.wait()


def per_device(
    current, previous, prev_coupling, mass_diag, near_blocks, near_cols,
    cluster_basis, coupling, send_list, far_slot,
):
    dma = pltpu.SemaphoreType.DMA
    vmem = pl.BlockSpec(memory_space=pltpu.VMEM)
    hbm = pl.BlockSpec(memory_space=pl.ANY)
    stack, mixed = pl.pallas_call(
        kernel,
        out_shape=(
            jax.ShapeDtypeStruct((64, ROWS), BF),
            jax.ShapeDtypeStruct((8, 128), F32),
        ),
        in_specs=[hbm] * 10,
        out_specs=(hbm, vmem),
        scratch_shapes=[
            pltpu.VMEM((NRHS, ROWS), F32),
            pltpu.VMEM((NRHS, ROWS), F32),
            pltpu.VMEM((NRHS, NRHS), F32),
            pltpu.VMEM((CPD, CL), F32),
            pltpu.VMEM((CPD * NNEAR, CL, CL), BF),
            pltpu.VMEM((CPD * RANK, CL), BF),
            pltpu.VMEM((CPD * RANK, NFAR * RANK), BF),
            pltpu.VMEM((CAP, 1, 128), jnp.int32),
            pltpu.VMEM((NNEAR, CPD), jnp.int32),
            pltpu.VMEM((NFAR, CPD), jnp.int32),
            pltpu.VMEM((3 * CPD, NRHS, CL), BF),
            pltpu.VMEM((64, ROWS), BF),
            pltpu.VMEM((NRHS, ROWS), F32),
            pltpu.VMEM((NRHS, ROWS), F32),
            pltpu.VMEM((TILES, NRHS, 128), BF),
            pltpu.VMEM((128, NRHS, 128), BF),
            pltpu.VMEM((128, NFAR * RANK), BF),
            pltpu.VMEM((1, 2048), jnp.int32),
            pltpu.SMEM((NNEAR, CPD), jnp.int32),
            pltpu.SMEM((NFAR, CPD), jnp.int32),
            pltpu.SMEM((1, 2048), jnp.int32),
            pltpu.VMEM((8, 8, 128), F32),
            pltpu.VMEM((16, 8, 128), F32),
            dma((9,)),
            dma((NEAR_CHUNKS,)),
            dma((3,)),
            dma,
            dma((9,)),
            dma((9,)),
            dma((9,)),
            dma((9,)),
            dma((36,)),
            dma((36,)),
            dma((10,)),
            dma((10,)),
            dma((39,)),
            dma((39,)),
            dma((2,)),
            dma((2,)),
            dma((22,)),
            dma((22,)),
        ],
        compiler_params=pltpu.CompilerParams(
            collective_id=0, has_side_effects=True, vmem_limit_bytes=56 << 20
        ),
    )(
        current,
        previous,
        prev_coupling,
        mass_diag.reshape(CPD, CL),
        near_blocks.reshape(CPD * NNEAR, CL, CL),
        near_cols.T,
        cluster_basis.reshape(CPD * RANK, CL),
        coupling.reshape(CPD * RANK, NFAR * RANK),
        send_list.transpose(2, 0, 1),
        far_slot.T,
    )
    return pl.pallas_call(
        finish,
        out_shape=(
            jax.ShapeDtypeStruct((NRHS, ROWS), F32),
            jax.ShapeDtypeStruct((NRHS, NRHS), F32),
            jax.ShapeDtypeStruct((NRHS, NRHS), F32),
        ),
        in_specs=[hbm, vmem],
        out_specs=(hbm, vmem, vmem),
        scratch_shapes=[
            pltpu.VMEM((64, ROWS), BF),
            pltpu.VMEM((NRHS, ROWS), F32),
            dma((2,)),
            dma((2,)),
        ],
    )(stack, mixed)


def solution(mesh):
    placed = (
        P(None, ("group", "sub")),
        P(None, ("group", "sub")),
        P(),
        P(("group", "sub")),
        P(("group", "sub"), None, None, None),
        P(("group", "sub"), None),
        P(("group", "sub"), None, None),
        P(("group", "sub"), None, None),
        P(("group", "sub"), None, None),
        P(("group", "sub"), None),
    )
    return jax.shard_map(
        per_device,
        mesh=mesh,
        in_specs=placed,
        out_specs=(P(None, ("group", "sub")), P(), P()),
        check_vma=False,
    )
```

```python
import functools

import jax
import jax.numpy as jnp
from jax import lax
from jax.experimental import pallas as pl
from jax.experimental.pallas import tpu as pltpu
from jax.sharding import PartitionSpec as P

MESH = pl.DeviceIdType.MESH
BF = jnp.bfloat16
F32 = jnp.float32
NRHS = 16
CL = 128
RANK = 24
NNEAR = 8
NFAR = 32
CAP = 12
CPD = 48
NCL = 6144
N = 786432
ROWS = CPD * CL
NGRP = CPD // 8
HIGHEST = lax.Precision.HIGHEST
PART_TILES = (4, 4, 2)
PART_BASE = (0, 512, 1024)
PER_TILE = 5
ORDERS = ((0, 1, 2), (2, 0, 1), (1, 2, 0))
OFFSETS = (2, 1, 3)
RELAY_UP, RELAY_DOWN = (0, 3), (1,)
XC = [(dx, dc) for dx in range(4) for dc in range(2) if dx or dc]
YZ = [(dy, dz) for dy in range(4) for dz in range(4) if dy or dz]
TILES = 1280
FAR_UNROLL = 6
NEAR_CHUNKS = 6


def nt(a, b, precision=None):
    return lax.dot_general(
        a, b, (((1,), (1,)), ((), ())), preferred_element_type=F32, precision=precision
    )


def tn(a, b, precision=None):
    return lax.dot_general(
        a, b, (((0,), (0,)), ((), ())), preferred_element_type=F32, precision=precision
    )


def nn(a, b, precision=None):
    return lax.dot_general(
        a, b, (((1,), (0,)), ((), ())), preferred_element_type=F32, precision=precision
    )


def split(x):
    hi = x.astype(BF)
    return hi, (x - hi.astype(F32)).astype(BF)


def kernel(
    cur_h, prev_h, pc_h, mass_h, near_h, ncol_h, basis_h, coup_h, slist_h, far_h,
    stack_h, mixed_ref,
    cur_v, prev_v, pc_v, mass_v, near_v, basis_v, coup_v, slist_v, ncol_v, far_v,
    win, stack, vbuf, ibuf, gathered, lists, xbuf,
    addr_v, ncol_s, far_s, addr_s,
    red_a, red_b,
    load_sem, near_sem, smem_sem, out_sem,
    p1_send, p1_recv, p2_send, p2_recv, p3_send, p3_recv, list_send, list_recv,
    sib_send, sib_recv, halo_send, halo_recv, red_send, red_recv,
):
    grp = lax.axis_index("group")
    sub = lax.axis_index("sub")
    me = grp * 16 + sub
    core = grp % 2
    pos = (sub % 4, grp // 2, sub // 4)

    def place(x, y, z, c):
        return (y * 2 + c, z * 4 + x)

    def shifted(axis, off):
        at = list(pos)
        at[axis] = (at[axis] + off) % 4
        return place(*at, core)

    def at_xc(dx, dc):
        return place((pos[0] + dx) % 4, pos[1], pos[2], (core + dc) % 2)

    def at_yz(dy, dz):
        return place(pos[0], (pos[1] + dy) % 4, (pos[2] + dz) % 4, core)

    sibling = place(*pos, 1 - core)

    def neighbour(off):
        d = (me + off) % 128
        return (d // 16, d % 16)

    loads = {}
    for n, (name, src, dst) in enumerate(
        (
            ("cur", cur_h, cur_v), ("basis", basis_h, basis_v), ("slist", slist_h, slist_v),
            ("ncol", ncol_h, ncol_v), ("far", far_h, far_v), ("pc", pc_h, pc_v),
            ("prev", prev_h, prev_v), ("mass", mass_h, mass_v), ("coup", coup_h, coup_v),
        )
    ):
        loads[name] = pltpu.make_async_copy(src, dst, load_sem.at[n])
        loads[name].start()
    per = CPD * NNEAR // NEAR_CHUNKS
    near_loads = []
    for n in range(NEAR_CHUNKS):
        part = pl.ds(n * per, per)
        copy = pltpu.make_async_copy(near_h.at[part], near_v.at[part], near_sem.at[n])
        copy.start()
        near_loads.append(copy)

    peers = [at_xc(dx, dc) for dx, dc in XC] + [at_yz(dy, dz) for dy, dz in YZ]
    peers += [neighbour(1), neighbour(127)]
    barrier = pltpu.get_barrier_semaphore()
    for d in peers:
        pl.semaphore_signal(barrier, inc=1, device_id=d, device_id_type=MESH)

    loads["cur"].wait()

    def window_step(c, _):
        cols = pl.ds(pl.multiple_of(c * CL, CL), CL)
        hi, lo = split(cur_v[:, cols])
        win[CPD + c] = hi
        stack[32:48, cols] = hi
        stack[48:64, cols] = lo
        return 0

    lax.fori_loop(0, CPD, window_step, 0, unroll=4)
    pl.semaphore_wait(barrier, len(peers))

    sends = []

    def put(src_ref, dst_ref, send_sem, recv_sem, device):
        copy = pltpu.make_async_remote_copy(
            src_ref=src_ref, dst_ref=dst_ref, send_sem=send_sem, recv_sem=recv_sem,
            device_id=device, device_id_type=MESH,
        )
        copy.start()
        sends.append(copy)
        return copy

    loads["basis"].wait()
    tiles = []
    for m in range(10):
        count = min(PER_TILE, CPD - m * PER_TILE)
        cl = win[CPD + m * PER_TILE : CPD + m * PER_TILE + count].reshape(count * NRHS, CL)
        y = nt(cl, basis_v[m * PER_TILE * RANK : (m * PER_TILE + count) * RANK, :])
        shape = (count * NRHS, count * RANK)
        diag = lax.broadcasted_iota(jnp.int32, shape, 0) // NRHS == (
            lax.broadcasted_iota(jnp.int32, shape, 1) // RANK
        )
        y = jnp.sum(jnp.where(diag, y, 0.0).reshape(count, NRHS, count * RANK), axis=0)
        y = jnp.concatenate([y, jnp.zeros((NRHS, 128 - count * RANK), F32)], axis=1)
        tiles.append(y.astype(BF))
    loads["slist"].wait()
    slist = slist_v[...].reshape(CAP, 128).astype(F32)
    slist = jnp.concatenate([slist, jnp.zeros((4, 128), F32)], axis=0).astype(BF)

    def chunk(p):
        at = [pos[a] for a in ORDERS[p]]
        first = ((core * 4 + at[2]) * 4 + at[1]) * 4 + at[0]
        return gathered.at[pl.ds(PART_BASE[p] + first * PART_TILES[p], PART_TILES[p])]

    def rows_of(p, k2, k3):
        at = [pos[a] for a in ORDERS[p]]
        first = (core * 4 + (at[2] + k3) % 4) * 4 + (at[1] + k2) % 4
        size = 4 * PART_TILES[p]
        return gathered.at[pl.ds(PART_BASE[p] + first * size, size)]

    def plane_of(p):
        size = 16 * PART_TILES[p]
        return gathered.at[pl.ds(PART_BASE[p] + (core * 4 + pos[ORDERS[p][2]]) * size, size)]

    def list_block(phase):
        first = core * 64 + pos[2] * 16
        if phase < 2:
            first = first + pos[1] * 4
        if phase < 1:
            first = first + pos[0]
        return lists.at[pl.ds(first, 4**phase)]

    done = 0
    for p in range(3):
        own = chunk(p)
        for i in range(PART_TILES[p]):
            own[i] = tiles[done + i]
        done += PART_TILES[p]
    list_block(0)[0] = slist

    def spread(ref, axis, sems, n):
        return {
            off: put(ref, ref, sems[0].at[n + k], sems[1].at[n + k], shifted(axis, off))
            for k, off in enumerate(OFFSETS)
        }

    def spread_list(phase):
        return spread(list_block(phase), phase, (list_send, list_recv), 3 * phase)

    def arrive(copies):
        for copy in copies.values():
            copy.wait_recv()

    sib_copies = []

    def to_sibling(ref):
        n = len(sib_copies)
        sib_copies.append(put(ref, ref, sib_send.at[n], sib_recv.at[n], sibling))

    phase3 = {}

    def start3(p, k2):
        axis = ORDERS[p][2]
        ref = rows_of(p, k2, 0)
        n = (p * 4 + k2) * 3
        phase3[p, k2] = copies = []
        if k2 not in RELAY_UP + RELAY_DOWN:
            copies.append(put(ref, ref, p3_send.at[n], p3_recv.at[n], shifted(axis, 2)))
        copies.append(put(ref, ref, p3_send.at[n + 1], p3_recv.at[n + 1], shifted(axis, 1)))
        copies.append(put(ref, ref, p3_send.at[n + 2], p3_recv.at[n + 2], shifted(axis, 3)))

    def relay3(k2):
        if k2 not in RELAY_UP + RELAY_DOWN:
            for p in range(3):
                phase3[p, k2][1].wait_recv()
                phase3[p, k2][2].wait_recv()
            return
        up = k2 in RELAY_UP
        for p in range(3):
            axis = ORDERS[p][2]
            n = (p * 4 + k2) * 3
            phase3[p, k2][0 if up else 1].wait_recv()
            ref = rows_of(p, k2, 3 if up else 1)
            copy = put(ref, ref, p3_send.at[n], p3_recv.at[n], shifted(axis, 1 if up else 3))
            phase3[p, k2].insert(0, copy)
        for p in range(3):
            phase3[p, k2][2 if up else 1].wait_recv()

    phase1 = [spread(chunk(p), ORDERS[p][0], (p1_send, p1_recv), 3 * p) for p in range(3)]
    lists1 = spread_list(0)

    mid = win.at[pl.ds(CPD, CPD)]
    halo = [
        put(mid, win.at[pl.ds(0, CPD)], halo_send.at[0], halo_recv.at[0], neighbour(1)),
        put(mid, win.at[pl.ds(2 * CPD, CPD)], halo_send.at[1], halo_recv.at[1], neighbour(127)),
    ]

    loads["ncol"].wait()
    wanted = ncol_v[...] - (me - 1) * CPD
    wanted = jnp.where(wanted < 0, wanted + NCL, wanted)
    wanted = jnp.where(wanted >= NCL, wanted - NCL, wanted)
    ncol_v[...] = jnp.clip(wanted, 0, 3 * CPD - 1)
    loads["far"].wait()
    q = far_v[...]
    src = (q * 43691) >> 19
    slot = q - src * CAP
    src_g, src_s = src >> 4, src & 15
    order = (src_g & 1) * 64 + (src_s >> 2) * 16 + (src_g >> 1) * 4 + (src_s & 3)
    far_v[...] = jnp.clip(order * 16 + slot, 0, 2047)
    ncol_copy = pltpu.make_async_copy(ncol_v, ncol_s, smem_sem.at[0])
    far_copy = pltpu.make_async_copy(far_v, far_s, smem_sem.at[1])
    ncol_copy.start()
    far_copy.start()

    loads["pc"].wait()
    loads["prev"].wait()
    pc = pc_v[...]
    pc_hi, pc_lo = split(pc)
    pc_rows = jnp.concatenate([pc_hi, pc_hi], axis=1)
    pc_rows2 = jnp.concatenate([pc_lo, pc_lo], axis=1)
    pc_all = jnp.concatenate([pc_rows, pc_rows2], axis=0)

    def previous_step(c, _):
        cols = pl.ds(pl.multiple_of(c * 512, 512), 512)
        hi, lo = split(prev_v[:, cols])
        both = nn(pc_all, jnp.concatenate([hi, lo], axis=0))
        vbuf[:, cols] = both[0:16] + both[16:32]
        return 0

    lax.fori_loop(0, ROWS // 512, previous_step, 0)

    for copies in phase1:
        arrive(copies)
    arrive(lists1)
    lists2 = spread_list(1)
    phase2 = [spread(rows_of(p, 0, 0), ORDERS[p][1], (p2_send, p2_recv), 3 * p) for p in range(3)]
    for p in range(3):
        start3(p, 0)
    loads["mass"].wait()
    loads["coup"].wait()
    ncol_copy.wait()
    far_copy.wait()
    arrive(lists2)
    lists3 = spread_list(2)
    for k2, off in ((1, 3), (3, 1), (2, 2)):
        if k2 == 2:
            relay3(0)
        for p in range(3):
            phase2[p][off].wait_recv()
            start3(p, k2)
    for p in range(3):
        to_sibling(plane_of(p))

    for copy in halo:
        copy.wait_recv()

    def near_step(r, _):
        xs, ms = [], []
        for j in range(NNEAR):
            w = ncol_s[j, r]
            xs.append(win[w])
        x = jnp.concatenate(xs, axis=1)
        m = near_v[pl.ds(r * NNEAR, NNEAR)]
        m = jnp.concatenate([m[j] for j in range(NNEAR)], axis=1)
        cols = pl.ds(pl.multiple_of(r * CL, CL), CL)
        ibuf[:, cols] = nt(x, m) + mass_v[pl.ds(r, 1), :] * cur_v[:, cols]
        return 0

    def near_chunk(n):
        rows_per = CPD // NEAR_CHUNKS
        near_loads[n].wait()
        lax.fori_loop(n * rows_per, (n + 1) * rows_per, near_step, 0, unroll=4)

    def forward3(k2):
        for p in range(3):
            to_sibling(rows_of(p, k2, 1))
            to_sibling(rows_of(p, k2, 3))

    near_chunk(0)
    arrive(lists3)
    list_plane = lists.at[pl.ds(core * 64, 64)]
    list_sib = put(list_plane, list_plane, list_send.at[9], list_recv.at[9], sibling)
    near_chunk(1)
    relay3(1)
    forward3(0)
    forward3(1)
    near_chunk(2)
    near_chunk(3)
    relay3(3)
    forward3(3)
    near_chunk(4)
    list_sib.wait_recv()

    mine = (lax.broadcasted_iota(jnp.int32, (16, 128), 1) == me).astype(BF)
    local = nt(mine, lists[...].reshape(2048, 128))[0:1]
    local = jnp.clip(local.astype(jnp.int32), 0, CPD - 1)
    t = lax.broadcasted_iota(jnp.int32, (1, 2048), 1) >> 4
    sx, sy, sz, sc = t & 3, (t >> 2) & 3, (t >> 4) & 3, t >> 6
    tile = (local * 13) >> 6
    at_a = (((sc * 4 + sz) * 4 + sy) * 4 + sx) * 4 + tile
    at_b = PART_BASE[1] + (((sc * 4 + sy) * 4 + sx) * 4 + sz) * 4 + tile - 4
    at_c = PART_BASE[2] + (((sc * 4 + sx) * 4 + sz) * 4 + sy) * 2 + tile - 8
    at = jnp.where(tile < 4, at_a, jnp.where(tile < 8, at_b, at_c))
    turn = (128 - (local - tile * PER_TILE) * RANK) & 127
    addr_v[...] = jnp.clip(at, 0, TILES - 1) * 128 + turn
    addr_copy = pltpu.make_async_copy(addr_v, addr_s, smem_sem.at[2])
    addr_copy.start()
    near_chunk(5)
    relay3(2)
    forward3(2)
    for k2 in (0, 1, 3, 2):
        for p in range(3):
            phase3[p, k2][0].wait_recv()
            to_sibling(rows_of(p, k2, 2))
    addr_copy.wait()
    for copy in sib_copies:
        copy.wait_recv()

    lane = lax.broadcasted_iota(jnp.int32, (16, 128), 1)
    diag = lax.broadcasted_iota(jnp.int32, (128, 8 * RANK), 0) // NRHS == (
        lax.broadcasted_iota(jnp.int32, (128, 8 * RANK), 1) // RANK
    )

    def far_step(i, total):
        for u in range(FAR_UNROLL):
            g = i * FAR_UNROLL + u
            for r in range(8):
                row = [None] * 6
                for j in range(NFAR):
                    word = addr_s[0, far_s[j, g * 8 + r]]
                    tile = pltpu.roll(gathered[word >> 7], (word + j * RANK) & 127, 1)
                    k, first = j * RANK // 128, j * RANK % 128
                    row[k] = tile if first == 0 else jnp.where(lane >= first, tile, row[k])
                    if first + RANK > 128:
                        row[k + 1] = tile
                xbuf[u, r * 16 : r * 16 + 16, :] = jnp.concatenate(row, axis=1)
            rows = pl.ds(pl.multiple_of(g * 192, 192), 192)
            combined = nt(xbuf[u], coup_v[rows, :])
            combined = jnp.where(diag, combined, 0.0).astype(BF)
            far = nn(combined, basis_v[rows, :])
            cols = pl.ds(pl.multiple_of(g * 1024, 1024), 1024)
            far = jnp.concatenate([far[r * 16 : r * 16 + 16] for r in range(8)], axis=1)
            image = ibuf[:, cols] + far
            j_hi, j_lo = split(image - vbuf[:, cols])
            i_hi, i_lo = split(image)
            stack[0:16, cols] = j_hi
            stack[16:32, cols] = j_lo
            s = jnp.concatenate([j_hi, j_lo, stack[32:64, cols]], axis=0)
            total = total + nt(s, jnp.concatenate([s, i_hi, i_lo], axis=0))
        return total

    inner = lax.fori_loop(0, NGRP // FAR_UNROLL, far_step, jnp.zeros((64, 96), F32))
    stack_copy = pltpu.make_async_copy(stack, stack_h, out_sem)
    stack_copy.start()

    inner = jnp.concatenate([inner, jnp.zeros((64, 32), F32)], axis=1)
    inner = inner + pltpu.roll(inner, 112, 1)
    j_rows = inner[0:16] + inner[16:32]
    c_rows = inner[32:48] + inner[48:64]
    mixed = jnp.where(lane < 48, c_rows, pltpu.roll(c_rows, 112, 1))
    mixed = jnp.where(lane < 32, pltpu.roll(c_rows, 16, 1), mixed)
    mixed = jnp.where(lane < 16, j_rows, mixed)
    mixed = jnp.where(lane[0:8] < 64, mixed[0:8], pltpu.roll(mixed[8:16], 64, 1))

    def reduce(value, buf, place_at, devices, n):
        buf[place_at] = value
        ref = buf.at[place_at]
        copies = [
            put(ref, ref, red_send.at[n + k], red_recv.at[n + k], d) for k, d in enumerate(devices)
        ]
        for copy in copies:
            copy.wait_recv()
        parts = [buf[k] for k in range(len(devices) + 1)]
        while len(parts) > 1:
            parts = [a + b for a, b in zip(parts[::2], parts[1::2])]
        return parts[0]

    mixed = reduce(mixed, red_a, pos[0] * 2 + core, [at_xc(*o) for o in XC], 0)
    mixed = reduce(mixed, red_b, pos[1] * 4 + pos[2], [at_yz(*o) for o in YZ], 7)
    mixed_ref[...] = mixed * (1.0 / N)
    stack_copy.wait()
    for copy in sends:
        copy.wait_send()


def finish(stack_h, mixed_ref, out_h, proj_ref, tri_ref, stack, out_v, load_sem, out_sem):
    half = ROWS // 2
    loads = []
    for n in range(2):
        part = pl.ds(n * half, half)
        loads.append(
            pltpu.make_async_copy(stack_h.at[:, part], stack.at[:, part], load_sem.at[n])
        )
        loads[n].start()
    mixed = mixed_ref[...]
    mixed = jnp.concatenate([mixed, pltpu.roll(mixed, 64, 1)], axis=0)
    row_id = lax.broadcasted_iota(jnp.int32, (16, 128), 0)
    lane_id = lax.broadcasted_iota(jnp.int32, (16, 128), 1)
    jj, cj, cc, proj = mixed[:, 0:16], mixed[:, 16:32], mixed[:, 32:48], mixed[:, 48:64]
    proj_ref[...] = proj
    both = tn(proj, mixed[:, 16:48], HIGHEST)
    gram = jj - both[:, 0:16] - nn(cj.T - both[:, 16:32], proj, HIGHEST)

    eye = (lane_id[:, 0:16] == row_id[:, 0:16]).astype(F32)
    m = jnp.concatenate([gram, eye, jnp.zeros((16, 96), F32)], axis=1)
    for k in range(16):
        pivot_row = jnp.broadcast_to(m[k : k + 1, :], (16, 128))
        pivot = m[k : k + 1, k : k + 1]
        factor = jnp.broadcast_to(m[:, k : k + 1] / pivot, (16, 128))
        m = m - jnp.where(row_id > k, factor, 0.0) * pivot_row
    d = jnp.sum(jnp.where(lane_id == row_id, m, 0.0), axis=1, keepdims=True)
    m = m / jnp.sqrt(d)
    upper = jnp.where(lane_id[:, 0:16] >= row_id[:, 0:16], m[:, 0:16], 0.0)
    tri_ref[...] = upper.T
    inverse = m[:, 16:32]
    m2 = -nt(inverse, proj, HIGHEST)
    m1_hi, m1_lo = split(inverse)
    m2_hi, m2_lo = split(m2)
    lhs = jnp.concatenate(
        [
            jnp.concatenate([m1_hi, m1_hi, m2_hi, m2_hi], axis=1),
            jnp.concatenate([m1_lo, m1_lo, m2_lo, m2_lo], axis=1),
        ],
        axis=0,
    )

    def out_step(c, _):
        cols = pl.ds(pl.multiple_of(c * 1024, 1024), 1024)
        both = nn(lhs, stack[:, cols])
        out_v[:, cols] = both[0:16] + both[16:32]
        return 0

    stores = []
    for n in range(2):
        part = pl.ds(n * half, half)
        loads[n].wait()
        lax.fori_loop(n * 3, n * 3 + 3, out_step, 0, unroll=3)
        stores.append(pltpu.make_async_copy(out_v.at[:, part], out_h.at[:, part], out_sem.at[n]))
        stores[n].start()
    for copy in stores:
        copy.wait()


def per_device(
    current, previous, prev_coupling, mass_diag, near_blocks, near_cols,
    cluster_basis, coupling, send_list, far_slot,
):
    dma = pltpu.SemaphoreType.DMA
    vmem = pl.BlockSpec(memory_space=pltpu.VMEM)
    hbm = pl.BlockSpec(memory_space=pl.ANY)
    stack, mixed = pl.pallas_call(
        kernel,
        out_shape=(
            jax.ShapeDtypeStruct((64, ROWS), BF),
            jax.ShapeDtypeStruct((8, 128), F32),
        ),
        in_specs=[hbm] * 10,
        out_specs=(hbm, vmem),
        scratch_shapes=[
            pltpu.VMEM((NRHS, ROWS), F32),
            pltpu.VMEM((NRHS, ROWS), F32),
            pltpu.VMEM((NRHS, NRHS), F32),
            pltpu.VMEM((CPD, CL), F32),
            pltpu.VMEM((CPD * NNEAR, CL, CL), BF),
            pltpu.VMEM((CPD * RANK, CL), BF),
            pltpu.VMEM((CPD * RANK, NFAR * RANK), BF),
            pltpu.VMEM((CAP, 1, 128), jnp.int32),
            pltpu.VMEM((NNEAR, CPD), jnp.int32),
            pltpu.VMEM((NFAR, CPD), jnp.int32),
            pltpu.VMEM((3 * CPD, NRHS, CL), BF),
            pltpu.VMEM((64, ROWS), BF),
            pltpu.VMEM((NRHS, ROWS), F32),
            pltpu.VMEM((NRHS, ROWS), F32),
            pltpu.VMEM((TILES, NRHS, 128), BF),
            pltpu.VMEM((128, NRHS, 128), BF),
            pltpu.VMEM((FAR_UNROLL, 128, NFAR * RANK), BF),
            pltpu.VMEM((1, 2048), jnp.int32),
            pltpu.SMEM((NNEAR, CPD), jnp.int32),
            pltpu.SMEM((NFAR, CPD), jnp.int32),
            pltpu.SMEM((1, 2048), jnp.int32),
            pltpu.VMEM((8, 8, 128), F32),
            pltpu.VMEM((16, 8, 128), F32),
            dma((9,)),
            dma((NEAR_CHUNKS,)),
            dma((3,)),
            dma,
            dma((9,)),
            dma((9,)),
            dma((9,)),
            dma((9,)),
            dma((36,)),
            dma((36,)),
            dma((10,)),
            dma((10,)),
            dma((39,)),
            dma((39,)),
            dma((2,)),
            dma((2,)),
            dma((22,)),
            dma((22,)),
        ],
        compiler_params=pltpu.CompilerParams(
            collective_id=0, has_side_effects=True, vmem_limit_bytes=56 << 20
        ),
    )(
        current,
        previous,
        prev_coupling,
        mass_diag.reshape(CPD, CL),
        near_blocks.reshape(CPD * NNEAR, CL, CL),
        near_cols.T,
        cluster_basis.reshape(CPD * RANK, CL),
        coupling.reshape(CPD * RANK, NFAR * RANK),
        send_list.transpose(2, 0, 1),
        far_slot.T,
    )
    return pl.pallas_call(
        finish,
        out_shape=(
            jax.ShapeDtypeStruct((NRHS, ROWS), F32),
            jax.ShapeDtypeStruct((NRHS, NRHS), F32),
            jax.ShapeDtypeStruct((NRHS, NRHS), F32),
        ),
        in_specs=[hbm, vmem],
        out_specs=(hbm, vmem, vmem),
        scratch_shapes=[
            pltpu.VMEM((64, ROWS), BF),
            pltpu.VMEM((NRHS, ROWS), F32),
            dma((2,)),
            dma((2,)),
        ],
    )(stack, mixed)


def solution(mesh):
    placed = (
        P(None, ("group", "sub")),
        P(None, ("group", "sub")),
        P(),
        P(("group", "sub")),
        P(("group", "sub"), None, None, None),
        P(("group", "sub"), None),
        P(("group", "sub"), None, None),
        P(("group", "sub"), None, None),
        P(("group", "sub"), None, None),
        P(("group", "sub"), None),
    )
    return jax.shard_map(
        per_device,
        mesh=mesh,
        in_specs=placed,
        out_specs=(P(None, ("group", "sub")), P(), P()),
        check_vma=False,
    )
```

```python
import functools

import jax
import jax.numpy as jnp
from jax import lax
from jax.experimental import pallas as pl
from jax.experimental.pallas import tpu as pltpu
from jax.sharding import PartitionSpec as P

MESH = pl.DeviceIdType.MESH
BF = jnp.bfloat16
F32 = jnp.float32
NRHS = 16
CL = 128
RANK = 24
NNEAR = 8
NFAR = 32
CAP = 12
CPD = 48
NCL = 6144
N = 786432
ROWS = CPD * CL
NGRP = CPD // 8
HIGHEST = lax.Precision.HIGHEST
PART_TILES = (3, 4, 3)
PART_BASE = (0, 384, 896)
PER_TILE = 5
ORDERS = ((0, 1, 2), (2, 0, 1), (1, 2, 0))
OFFSETS = (2, 1, 3)
RELAY_UP, RELAY_DOWN = (0, 3), (1,)
XC = [(2, 0), (2, 1), (1, 0), (3, 0), (1, 1), (3, 1), (0, 1)]
YZ = sorted([(dy, dz) for dy in range(4) for dz in range(4) if dy or dz], key=lambda o: -(min(o[0], 4 - o[0]) + min(o[1], 4 - o[1])))
TILES = 1280
FAR_UNROLL = 6
NEAR_CHUNKS = 6


def nt(a, b, precision=None):
    return lax.dot_general(
        a, b, (((1,), (1,)), ((), ())), preferred_element_type=F32, precision=precision
    )


def tn(a, b, precision=None):
    return lax.dot_general(
        a, b, (((0,), (0,)), ((), ())), preferred_element_type=F32, precision=precision
    )


def nn(a, b, precision=None):
    return lax.dot_general(
        a, b, (((1,), (0,)), ((), ())), preferred_element_type=F32, precision=precision
    )


def split(x):
    hi = x.astype(BF)
    return hi, (x - hi.astype(F32)).astype(BF)


def kernel(
    cur_h, prev_h, pc_h, mass_h, near_h, ncol_h, basis_h, coup_h, slist_h, far_h,
    stack_h, mixed_ref,
    cur_v, prev_v, pc_v, mass_v, near_v, basis_v, coup_v, slist_v, ncol_v, far_v,
    win, stack, vbuf, ibuf, gathered, lists, xbuf,
    addr_v, ncol_s, far_s, addr_s,
    red_a, red_b,
    load_sem, near_sem, smem_sem, out_sem,
    p1_send, p1_recv, p2_send, p2_recv, p3_send, p3_recv, list_send, list_recv,
    sib_send, sib_recv, halo_send, halo_recv, red_send, red_recv,
):
    grp = lax.axis_index("group")
    sub = lax.axis_index("sub")
    me = grp * 16 + sub
    core = grp % 2
    pos = (sub % 4, grp // 2, sub // 4)

    def place(x, y, z, c):
        return (y * 2 + c, z * 4 + x)

    def shifted(axis, off):
        at = list(pos)
        at[axis] = (at[axis] + off) % 4
        return place(*at, core)

    def at_xc(dx, dc):
        return place((pos[0] + dx) % 4, pos[1], pos[2], (core + dc) % 2)

    def at_yz(dy, dz):
        return place(pos[0], (pos[1] + dy) % 4, (pos[2] + dz) % 4, core)

    sibling = place(*pos, 1 - core)

    def neighbour(off):
        d = (me + off) % 128
        return (d // 16, d % 16)

    loads = {}
    for n, (name, src, dst) in enumerate(
        (
            ("cur", cur_h, cur_v), ("basis", basis_h, basis_v), ("slist", slist_h, slist_v),
            ("ncol", ncol_h, ncol_v), ("far", far_h, far_v), ("pc", pc_h, pc_v),
            ("prev", prev_h, prev_v), ("mass", mass_h, mass_v), ("coup", coup_h, coup_v),
        )
    ):
        loads[name] = pltpu.make_async_copy(src, dst, load_sem.at[n])
        loads[name].start()
    per = CPD * NNEAR // NEAR_CHUNKS
    near_loads = []
    for n in range(NEAR_CHUNKS):
        part = pl.ds(n * per, per)
        copy = pltpu.make_async_copy(near_h.at[part], near_v.at[part], near_sem.at[n])
        copy.start()
        near_loads.append(copy)

    peers = [at_xc(dx, dc) for dx, dc in XC] + [at_yz(dy, dz) for dy, dz in YZ]
    peers += [neighbour(1), neighbour(127)]
    barrier = pltpu.get_barrier_semaphore()
    for d in peers:
        pl.semaphore_signal(barrier, inc=1, device_id=d, device_id_type=MESH)

    loads["cur"].wait()

    def window_step(c, _):
        cols = pl.ds(pl.multiple_of(c * CL, CL), CL)
        hi, lo = split(cur_v[:, cols])
        win[CPD + c] = hi
        stack[32:48, cols] = hi
        stack[48:64, cols] = lo
        return 0

    lax.fori_loop(0, CPD, window_step, 0, unroll=4)
    pl.semaphore_wait(barrier, len(peers))

    sends = []

    def put(src_ref, dst_ref, send_sem, recv_sem, device):
        copy = pltpu.make_async_remote_copy(
            src_ref=src_ref, dst_ref=dst_ref, send_sem=send_sem, recv_sem=recv_sem,
            device_id=device, device_id_type=MESH,
        )
        copy.start()
        sends.append(copy)
        return copy

    loads["basis"].wait()
    tiles = []
    for m in range(10):
        count = min(PER_TILE, CPD - m * PER_TILE)
        cl = win[CPD + m * PER_TILE : CPD + m * PER_TILE + count].reshape(count * NRHS, CL)
        y = nt(cl, basis_v[m * PER_TILE * RANK : (m * PER_TILE + count) * RANK, :])
        shape = (count * NRHS, count * RANK)
        diag = lax.broadcasted_iota(jnp.int32, shape, 0) // NRHS == (
            lax.broadcasted_iota(jnp.int32, shape, 1) // RANK
        )
        y = jnp.sum(jnp.where(diag, y, 0.0).reshape(count, NRHS, count * RANK), axis=0)
        y = jnp.concatenate([y, jnp.zeros((NRHS, 128 - count * RANK), F32)], axis=1)
        tiles.append(y.astype(BF))
    loads["slist"].wait()
    slist = slist_v[...].reshape(CAP, 128).astype(F32)
    slist = jnp.concatenate([slist, jnp.zeros((4, 128), F32)], axis=0).astype(BF)

    def chunk(p):
        at = [pos[a] for a in ORDERS[p]]
        first = ((core * 4 + at[2]) * 4 + at[1]) * 4 + at[0]
        return gathered.at[pl.ds(PART_BASE[p] + first * PART_TILES[p], PART_TILES[p])]

    def rows_of(p, k2, k3):
        at = [pos[a] for a in ORDERS[p]]
        first = (core * 4 + (at[2] + k3) % 4) * 4 + (at[1] + k2) % 4
        size = 4 * PART_TILES[p]
        return gathered.at[pl.ds(PART_BASE[p] + first * size, size)]

    def plane_of(p):
        size = 16 * PART_TILES[p]
        return gathered.at[pl.ds(PART_BASE[p] + (core * 4 + pos[ORDERS[p][2]]) * size, size)]

    def list_block(phase):
        first = core * 64 + pos[2] * 16
        if phase < 2:
            first = first + pos[1] * 4
        if phase < 1:
            first = first + pos[0]
        return lists.at[pl.ds(first, 4**phase)]

    done = 0
    for p in range(3):
        own = chunk(p)
        for i in range(PART_TILES[p]):
            own[i] = tiles[done + i]
        done += PART_TILES[p]
    list_block(0)[0] = slist

    def spread(ref, axis, sems, n):
        return {
            off: put(ref, ref, sems[0].at[n + k], sems[1].at[n + k], shifted(axis, off))
            for k, off in enumerate(OFFSETS)
        }

    def spread_list(phase):
        return spread(list_block(phase), phase, (list_send, list_recv), 3 * phase)

    def arrive(copies):
        for copy in copies.values():
            copy.wait_recv()

    sib_copies = []

    def to_sibling(ref):
        n = len(sib_copies)
        sib_copies.append(put(ref, ref, sib_send.at[n], sib_recv.at[n], sibling))

    phase3 = {}

    def start3(p, k2):
        axis = ORDERS[p][2]
        ref = rows_of(p, k2, 0)
        n = (p * 4 + k2) * 3
        phase3[p, k2] = copies = []
        if k2 not in RELAY_UP + RELAY_DOWN:
            copies.append(put(ref, ref, p3_send.at[n], p3_recv.at[n], shifted(axis, 2)))
        copies.append(put(ref, ref, p3_send.at[n + 1], p3_recv.at[n + 1], shifted(axis, 1)))
        copies.append(put(ref, ref, p3_send.at[n + 2], p3_recv.at[n + 2], shifted(axis, 3)))

    def relay3(k2):
        if k2 not in RELAY_UP + RELAY_DOWN:
            for p in range(3):
                phase3[p, k2][1].wait_recv()
                phase3[p, k2][2].wait_recv()
            return
        up = k2 in RELAY_UP
        for p in range(3):
            axis = ORDERS[p][2]
            n = (p * 4 + k2) * 3
            phase3[p, k2][0 if up else 1].wait_recv()
            ref = rows_of(p, k2, 3 if up else 1)
            copy = put(ref, ref, p3_send.at[n], p3_recv.at[n], shifted(axis, 1 if up else 3))
            phase3[p, k2].insert(0, copy)
        for p in range(3):
            phase3[p, k2][2 if up else 1].wait_recv()

    phase1 = [spread(chunk(p), ORDERS[p][0], (p1_send, p1_recv), 3 * p) for p in range(3)]
    lists1 = spread_list(0)

    mid = win.at[pl.ds(CPD, CPD)]
    halo = [
        put(mid, win.at[pl.ds(0, CPD)], halo_send.at[0], halo_recv.at[0], neighbour(1)),
        put(mid, win.at[pl.ds(2 * CPD, CPD)], halo_send.at[1], halo_recv.at[1], neighbour(127)),
    ]

    loads["ncol"].wait()
    wanted = ncol_v[...] - (me - 1) * CPD
    wanted = jnp.where(wanted < 0, wanted + NCL, wanted)
    wanted = jnp.where(wanted >= NCL, wanted - NCL, wanted)
    ncol_v[...] = jnp.clip(wanted, 0, 3 * CPD - 1)
    loads["far"].wait()
    q = far_v[...]
    src = (q * 43691) >> 19
    slot = q - src * CAP
    src_g, src_s = src >> 4, src & 15
    order = (src_g & 1) * 64 + (src_s >> 2) * 16 + (src_g >> 1) * 4 + (src_s & 3)
    far_v[...] = jnp.clip(order * 16 + slot, 0, 2047)
    ncol_copy = pltpu.make_async_copy(ncol_v, ncol_s, smem_sem.at[0])
    far_copy = pltpu.make_async_copy(far_v, far_s, smem_sem.at[1])
    ncol_copy.start()
    far_copy.start()

    loads["pc"].wait()
    loads["prev"].wait()
    pc = pc_v[...]
    pc_hi, pc_lo = split(pc)
    pc_rows = jnp.concatenate([pc_hi, pc_hi], axis=1)
    pc_rows2 = jnp.concatenate([pc_lo, pc_lo], axis=1)
    pc_all = jnp.concatenate([pc_rows, pc_rows2], axis=0)

    def previous_step(c, _):
        cols = pl.ds(pl.multiple_of(c * 512, 512), 512)
        hi, lo = split(prev_v[:, cols])
        both = nn(pc_all, jnp.concatenate([hi, lo], axis=0))
        vbuf[:, cols] = both[0:16] + both[16:32]
        return 0

    lax.fori_loop(0, ROWS // 512, previous_step, 0)

    for copies in phase1:
        arrive(copies)
    arrive(lists1)
    lists2 = spread_list(1)
    phase2 = [spread(rows_of(p, 0, 0), ORDERS[p][1], (p2_send, p2_recv), 3 * p) for p in range(3)]
    for p in range(3):
        start3(p, 0)
    loads["mass"].wait()
    loads["coup"].wait()
    ncol_copy.wait()
    far_copy.wait()
    arrive(lists2)
    lists3 = spread_list(2)
    for k2, off in ((1, 3), (3, 1), (2, 2)):
        if k2 == 2:
            relay3(0)
        for p in range(3):
            phase2[p][off].wait_recv()
            start3(p, k2)
    for p in range(3):
        to_sibling(plane_of(p))

    for copy in halo:
        copy.wait_recv()

    def near_step(r, _):
        xs, ms = [], []
        for j in range(NNEAR):
            w = ncol_s[j, r]
            xs.append(win[w])
        x = jnp.concatenate(xs, axis=1)
        m = near_v[pl.ds(r * NNEAR, NNEAR)]
        m = jnp.concatenate([m[j] for j in range(NNEAR)], axis=1)
        cols = pl.ds(pl.multiple_of(r * CL, CL), CL)
        ibuf[:, cols] = nt(x, m) + mass_v[pl.ds(r, 1), :] * cur_v[:, cols]
        return 0

    def near_chunk(n):
        rows_per = CPD // NEAR_CHUNKS
        near_loads[n].wait()
        lax.fori_loop(n * rows_per, (n + 1) * rows_per, near_step, 0, unroll=8)

    def forward3(k2):
        for p in range(3):
            to_sibling(rows_of(p, k2, 1))
            to_sibling(rows_of(p, k2, 3))

    near_chunk(0)
    arrive(lists3)
    list_plane = lists.at[pl.ds(core * 64, 64)]
    list_sib = put(list_plane, list_plane, list_send.at[9], list_recv.at[9], sibling)
    near_chunk(1)
    relay3(1)
    forward3(0)
    forward3(1)
    near_chunk(2)
    near_chunk(3)
    relay3(3)
    forward3(3)
    near_chunk(4)
    list_sib.wait_recv()

    mine = (lax.broadcasted_iota(jnp.int32, (16, 128), 1) == me).astype(BF)
    local = nt(mine, lists[...].reshape(2048, 128))[0:1]
    local = jnp.clip(local.astype(jnp.int32), 0, CPD - 1)
    t = lax.broadcasted_iota(jnp.int32, (1, 2048), 1) >> 4
    sx, sy, sz, sc = t & 3, (t >> 2) & 3, (t >> 4) & 3, t >> 6
    tile = (local * 13) >> 6
    at_a = (((sc * 4 + sz) * 4 + sy) * 4 + sx) * 3 + tile
    at_b = PART_BASE[1] + (((sc * 4 + sy) * 4 + sx) * 4 + sz) * 4 + tile - 3
    at_c = PART_BASE[2] + (((sc * 4 + sx) * 4 + sz) * 4 + sy) * 3 + tile - 7
    at = jnp.where(tile < 3, at_a, jnp.where(tile < 7, at_b, at_c))
    turn = (128 - (local - tile * PER_TILE) * RANK) & 127
    addr_v[...] = jnp.clip(at, 0, TILES - 1) * 128 + turn
    addr_copy = pltpu.make_async_copy(addr_v, addr_s, smem_sem.at[2])
    addr_copy.start()
    near_chunk(5)
    relay3(2)
    forward3(2)
    for k2 in (0, 1, 3, 2):
        for p in range(3):
            phase3[p, k2][0].wait_recv()
            to_sibling(rows_of(p, k2, 2))
    addr_copy.wait()
    for copy in sib_copies:
        copy.wait_recv()

    lane = lax.broadcasted_iota(jnp.int32, (16, 128), 1)
    diag = lax.broadcasted_iota(jnp.int32, (128, 8 * RANK), 0) // NRHS == (
        lax.broadcasted_iota(jnp.int32, (128, 8 * RANK), 1) // RANK
    )

    def far_step(i, total):
        for u in range(FAR_UNROLL):
            g = i * FAR_UNROLL + u
            for r in range(8):
                row = [None] * 6
                for j in range(NFAR):
                    word = addr_s[0, far_s[j, g * 8 + r]]
                    tile = pltpu.roll(gathered[word >> 7], (word + j * RANK) & 127, 1)
                    k, first = j * RANK // 128, j * RANK % 128
                    row[k] = tile if first == 0 else jnp.where(lane >= first, tile, row[k])
                    if first + RANK > 128:
                        row[k + 1] = tile
                xbuf[u, r * 16 : r * 16 + 16, :] = jnp.concatenate(row, axis=1)
            rows = pl.ds(pl.multiple_of(g * 192, 192), 192)
            combined = nt(xbuf[u], coup_v[rows, :])
            combined = jnp.where(diag, combined, 0.0).astype(BF)
            far = nn(combined, basis_v[rows, :])
            cols = pl.ds(pl.multiple_of(g * 1024, 1024), 1024)
            far = jnp.concatenate([far[r * 16 : r * 16 + 16] for r in range(8)], axis=1)
            image = ibuf[:, cols] + far
            j_hi, j_lo = split(image - vbuf[:, cols])
            i_hi, i_lo = split(image)
            stack[0:16, cols] = j_hi
            stack[16:32, cols] = j_lo
            s = jnp.concatenate([j_hi, j_lo, stack[32:64, cols]], axis=0)
            total = total + nt(s, jnp.concatenate([s, i_hi, i_lo], axis=0))
        return total

    inner = lax.fori_loop(0, NGRP // FAR_UNROLL, far_step, jnp.zeros((64, 96), F32))
    stack_copy = pltpu.make_async_copy(stack, stack_h, out_sem)
    stack_copy.start()

    inner = jnp.concatenate([inner, jnp.zeros((64, 32), F32)], axis=1)
    inner = inner + pltpu.roll(inner, 112, 1)
    j_rows = inner[0:16] + inner[16:32]
    c_rows = inner[32:48] + inner[48:64]
    mixed = jnp.where(lane < 48, c_rows, pltpu.roll(c_rows, 112, 1))
    mixed = jnp.where(lane < 32, pltpu.roll(c_rows, 16, 1), mixed)
    mixed = jnp.where(lane < 16, j_rows, mixed)
    mixed = jnp.where(lane[0:8] < 64, mixed[0:8], pltpu.roll(mixed[8:16], 64, 1))

    def reduce(value, buf, place_at, devices, n):
        buf[place_at] = value
        ref = buf.at[place_at]
        copies = [
            put(ref, ref, red_send.at[n + k], red_recv.at[n + k], d) for k, d in enumerate(devices)
        ]
        for copy in copies:
            copy.wait_recv()
        parts = [buf[k] for k in range(len(devices) + 1)]
        while len(parts) > 1:
            parts = [a + b for a, b in zip(parts[::2], parts[1::2])]
        return parts[0]

    mixed = reduce(mixed, red_a, pos[0] * 2 + core, [at_xc(*o) for o in XC], 0)
    mixed = reduce(mixed, red_b, pos[1] * 4 + pos[2], [at_yz(*o) for o in YZ], 7)
    mixed_ref[...] = mixed * (1.0 / N)
    stack_copy.wait()
    for copy in sends:
        copy.wait_send()


def finish(stack_h, mixed_ref, out_h, proj_ref, tri_ref, stack, out_v, load_sem, out_sem):
    half = ROWS // 2
    loads = []
    for n in range(2):
        part = pl.ds(n * half, half)
        loads.append(
            pltpu.make_async_copy(stack_h.at[:, part], stack.at[:, part], load_sem.at[n])
        )
        loads[n].start()
    mixed = mixed_ref[...]
    mixed = jnp.concatenate([mixed, pltpu.roll(mixed, 64, 1)], axis=0)
    row_id = lax.broadcasted_iota(jnp.int32, (16, 128), 0)
    lane_id = lax.broadcasted_iota(jnp.int32, (16, 128), 1)
    jj, cj, cc, proj = mixed[:, 0:16], mixed[:, 16:32], mixed[:, 32:48], mixed[:, 48:64]
    proj_ref[...] = proj
    left = jnp.concatenate([proj, cj], axis=0)
    right = jnp.concatenate([cj - nn(cc, proj, HIGHEST), proj], axis=0)
    gram = jj - tn(left, right, HIGHEST)

    eye = (lane_id[:, 0:16] == row_id[:, 0:16]).astype(F32)
    minus = -proj.T
    m = jnp.concatenate([gram, eye, eye, minus, minus, jnp.zeros((16, 48), F32)], axis=1)
    for k in range(16):
        pivot_row = jnp.broadcast_to(m[k : k + 1, :], (16, 128))
        pivot = m[k : k + 1, k : k + 1]
        factor = jnp.broadcast_to(m[:, k : k + 1] / pivot, (16, 128))
        m = m - jnp.where(row_id > k, factor, 0.0) * pivot_row
    d = jnp.sum(jnp.where(lane_id == row_id, m, 0.0), axis=1, keepdims=True)
    m = m / jnp.sqrt(d)
    upper = jnp.where(lane_id[:, 0:16] >= row_id[:, 0:16], m[:, 0:16], 0.0)
    tri_ref[...] = upper.T
    hi, lo = split(m[:, 16:80])
    lhs = jnp.concatenate([hi, lo], axis=0)

    def out_step(c, _):
        cols = pl.ds(pl.multiple_of(c * 1024, 1024), 1024)
        both = nn(lhs, stack[:, cols])
        out_v[:, cols] = both[0:16] + both[16:32]
        return 0

    stores = []
    for n in range(2):
        part = pl.ds(n * half, half)
        loads[n].wait()
        lax.fori_loop(n * 3, n * 3 + 3, out_step, 0, unroll=3)
        stores.append(pltpu.make_async_copy(out_v.at[:, part], out_h.at[:, part], out_sem.at[n]))
        stores[n].start()
    for copy in stores:
        copy.wait()


def per_device(
    current, previous, prev_coupling, mass_diag, near_blocks, near_cols,
    cluster_basis, coupling, send_list, far_slot,
):
    dma = pltpu.SemaphoreType.DMA
    vmem = pl.BlockSpec(memory_space=pltpu.VMEM)
    hbm = pl.BlockSpec(memory_space=pl.ANY)
    stack, mixed = pl.pallas_call(
        kernel,
        out_shape=(
            jax.ShapeDtypeStruct((64, ROWS), BF),
            jax.ShapeDtypeStruct((8, 128), F32),
        ),
        in_specs=[hbm] * 10,
        out_specs=(hbm, vmem),
        scratch_shapes=[
            pltpu.VMEM((NRHS, ROWS), F32),
            pltpu.VMEM((NRHS, ROWS), F32),
            pltpu.VMEM((NRHS, NRHS), F32),
            pltpu.VMEM((CPD, CL), F32),
            pltpu.VMEM((CPD * NNEAR, CL, CL), BF),
            pltpu.VMEM((CPD * RANK, CL), BF),
            pltpu.VMEM((CPD * RANK, NFAR * RANK), BF),
            pltpu.VMEM((CAP, 1, 128), jnp.int32),
            pltpu.VMEM((NNEAR, CPD), jnp.int32),
            pltpu.VMEM((NFAR, CPD), jnp.int32),
            pltpu.VMEM((3 * CPD, NRHS, CL), BF),
            pltpu.VMEM((64, ROWS), BF),
            pltpu.VMEM((NRHS, ROWS), F32),
            pltpu.VMEM((NRHS, ROWS), F32),
            pltpu.VMEM((TILES, NRHS, 128), BF),
            pltpu.VMEM((128, NRHS, 128), BF),
            pltpu.VMEM((FAR_UNROLL, 128, NFAR * RANK), BF),
            pltpu.VMEM((1, 2048), jnp.int32),
            pltpu.SMEM((NNEAR, CPD), jnp.int32),
            pltpu.SMEM((NFAR, CPD), jnp.int32),
            pltpu.SMEM((1, 2048), jnp.int32),
            pltpu.VMEM((8, 8, 128), F32),
            pltpu.VMEM((16, 8, 128), F32),
            dma((9,)),
            dma((NEAR_CHUNKS,)),
            dma((3,)),
            dma,
            dma((9,)),
            dma((9,)),
            dma((9,)),
            dma((9,)),
            dma((36,)),
            dma((36,)),
            dma((10,)),
            dma((10,)),
            dma((39,)),
            dma((39,)),
            dma((2,)),
            dma((2,)),
            dma((22,)),
            dma((22,)),
        ],
        compiler_params=pltpu.CompilerParams(
            collective_id=0, has_side_effects=True, vmem_limit_bytes=56 << 20
        ),
    )(
        current,
        previous,
        prev_coupling,
        mass_diag.reshape(CPD, CL),
        near_blocks.reshape(CPD * NNEAR, CL, CL),
        near_cols.T,
        cluster_basis.reshape(CPD * RANK, CL),
        coupling.reshape(CPD * RANK, NFAR * RANK),
        send_list.transpose(2, 0, 1),
        far_slot.T,
    )
    return pl.pallas_call(
        finish,
        out_shape=(
            jax.ShapeDtypeStruct((NRHS, ROWS), F32),
            jax.ShapeDtypeStruct((NRHS, NRHS), F32),
            jax.ShapeDtypeStruct((NRHS, NRHS), F32),
        ),
        in_specs=[hbm, vmem],
        out_specs=(hbm, vmem, vmem),
        scratch_shapes=[
            pltpu.VMEM((64, ROWS), BF),
            pltpu.VMEM((NRHS, ROWS), F32),
            dma((2,)),
            dma((2,)),
        ],
    )(stack, mixed)


def solution(mesh):
    placed = (
        P(None, ("group", "sub")),
        P(None, ("group", "sub")),
        P(),
        P(("group", "sub")),
        P(("group", "sub"), None, None, None),
        P(("group", "sub"), None),
        P(("group", "sub"), None, None),
        P(("group", "sub"), None, None),
        P(("group", "sub"), None, None),
        P(("group", "sub"), None),
    )
    return jax.shard_map(
        per_device,
        mesh=mesh,
        in_specs=placed,
        out_specs=(P(None, ("group", "sub")), P(), P()),
        check_vma=False,
    )
```

```python
import functools

import jax
import jax.numpy as jnp
from jax import lax
from jax.experimental import pallas as pl
from jax.experimental.pallas import tpu as pltpu
from jax.sharding import PartitionSpec as P

MESH = pl.DeviceIdType.MESH
BF = jnp.bfloat16
F32 = jnp.float32
NRHS = 16
CL = 128
RANK = 24
NNEAR = 8
NFAR = 32
CAP = 12
CPD = 48
NCL = 6144
N = 786432
ROWS = CPD * CL
NGRP = CPD // 8
HIGHEST = lax.Precision.HIGHEST
PART_TILES = (3, 4, 3)
PART_BASE = (0, 384, 896)
PER_TILE = 5
ORDERS = ((0, 1, 2), (2, 0, 1), (1, 2, 0))
OFFSETS = (2, 1, 3)
RELAY_UP, RELAY_DOWN = (0, 3), (1,)
XC = [(2, 0), (2, 1), (1, 0), (3, 0), (1, 1), (3, 1), (0, 1)]
YZ = sorted([(dy, dz) for dy in range(4) for dz in range(4) if dy or dz], key=lambda o: -(min(o[0], 4 - o[0]) + min(o[1], 4 - o[1])))
TILES = 1280
FAR_UNROLL = 6
NEAR_CHUNKS = 6


def nt(a, b, precision=None):
    return lax.dot_general(
        a, b, (((1,), (1,)), ((), ())), preferred_element_type=F32, precision=precision
    )


def tn(a, b, precision=None):
    return lax.dot_general(
        a, b, (((0,), (0,)), ((), ())), preferred_element_type=F32, precision=precision
    )


def nn(a, b, precision=None):
    return lax.dot_general(
        a, b, (((1,), (0,)), ((), ())), preferred_element_type=F32, precision=precision
    )


def split(x):
    hi = x.astype(BF)
    return hi, (x - hi.astype(F32)).astype(BF)


def kernel(
    cur_h, prev_h, pc_h, mass_h, near_h, ncol_h, basis_h, coup_h, slist_h, far_h,
    stack_h, mixed_ref,
    cur_v, prev_v, pc_v, mass_v, near_v, basis_v, coup_v, slist_v, ncol_v, far_v,
    win, stack, vbuf, ibuf, gathered, lists, xbuf,
    addr_v, ncol_s, far_s, addr_s,
    red_a, red_b,
    load_sem, near_sem, smem_sem, out_sem,
    p1_send, p1_recv, p2_send, p2_recv, p3_send, p3_recv, list_send, list_recv,
    sib_send, sib_recv, halo_send, halo_recv, red_send, red_recv,
):
    grp = lax.axis_index("group")
    sub = lax.axis_index("sub")
    me = grp * 16 + sub
    core = grp % 2
    pos = (sub % 4, grp // 2, sub // 4)

    def place(x, y, z, c):
        return (y * 2 + c, z * 4 + x)

    def shifted(axis, off):
        at = list(pos)
        at[axis] = (at[axis] + off) % 4
        return place(*at, core)

    def at_xc(dx, dc):
        return place((pos[0] + dx) % 4, pos[1], pos[2], (core + dc) % 2)

    def at_yz(dy, dz):
        return place(pos[0], (pos[1] + dy) % 4, (pos[2] + dz) % 4, core)

    sibling = place(*pos, 1 - core)

    def neighbour(off):
        d = (me + off) % 128
        return (d // 16, d % 16)

    peers = [at_xc(dx, dc) for dx, dc in XC] + [at_yz(dy, dz) for dy, dz in YZ]
    peers += [neighbour(1), neighbour(127)]
    barrier = pltpu.get_barrier_semaphore()
    for d in peers:
        pl.semaphore_signal(barrier, inc=1, device_id=d, device_id_type=MESH)

    loads = {}
    for n, (name, src, dst) in enumerate(
        (
            ("cur", cur_h, cur_v), ("basis", basis_h, basis_v), ("slist", slist_h, slist_v),
            ("ncol", ncol_h, ncol_v), ("far", far_h, far_v), ("pc", pc_h, pc_v),
            ("prev", prev_h, prev_v), ("mass", mass_h, mass_v), ("coup", coup_h, coup_v),
        )
    ):
        loads[name] = pltpu.make_async_copy(src, dst, load_sem.at[n])
        loads[name].start()
    per = CPD * NNEAR // NEAR_CHUNKS
    near_loads = []
    for n in range(NEAR_CHUNKS):
        part = pl.ds(n * per, per)
        copy = pltpu.make_async_copy(near_h.at[part], near_v.at[part], near_sem.at[n])
        copy.start()
        near_loads.append(copy)

    loads["cur"].wait()

    def window_step(c, _):
        cols = pl.ds(pl.multiple_of(c * CL, CL), CL)
        hi, lo = split(cur_v[:, cols])
        win[CPD + c] = hi
        stack[32:48, cols] = hi
        stack[48:64, cols] = lo
        return 0

    lax.fori_loop(0, CPD, window_step, 0, unroll=4)
    pl.semaphore_wait(barrier, len(peers))

    sends = []

    def put(src_ref, dst_ref, send_sem, recv_sem, device):
        copy = pltpu.make_async_remote_copy(
            src_ref=src_ref, dst_ref=dst_ref, send_sem=send_sem, recv_sem=recv_sem,
            device_id=device, device_id_type=MESH,
        )
        copy.start()
        sends.append(copy)
        return copy

    loads["basis"].wait()
    tiles = []
    for m in range(10):
        count = min(PER_TILE, CPD - m * PER_TILE)
        cl = win[CPD + m * PER_TILE : CPD + m * PER_TILE + count].reshape(count * NRHS, CL)
        y = nt(cl, basis_v[m * PER_TILE * RANK : (m * PER_TILE + count) * RANK, :])
        shape = (count * NRHS, count * RANK)
        diag = lax.broadcasted_iota(jnp.int32, shape, 0) // NRHS == (
            lax.broadcasted_iota(jnp.int32, shape, 1) // RANK
        )
        y = jnp.sum(jnp.where(diag, y, 0.0).reshape(count, NRHS, count * RANK), axis=0)
        y = jnp.concatenate([y, jnp.zeros((NRHS, 128 - count * RANK), F32)], axis=1)
        tiles.append(y.astype(BF))
    loads["slist"].wait()
    slist = slist_v[...].reshape(CAP, 128).astype(F32)
    slist = jnp.concatenate([slist, jnp.zeros((4, 128), F32)], axis=0).astype(BF)

    def chunk(p):
        at = [pos[a] for a in ORDERS[p]]
        first = ((core * 4 + at[2]) * 4 + at[1]) * 4 + at[0]
        return gathered.at[pl.ds(PART_BASE[p] + first * PART_TILES[p], PART_TILES[p])]

    def rows_of(p, k2, k3):
        at = [pos[a] for a in ORDERS[p]]
        first = (core * 4 + (at[2] + k3) % 4) * 4 + (at[1] + k2) % 4
        size = 4 * PART_TILES[p]
        return gathered.at[pl.ds(PART_BASE[p] + first * size, size)]

    def plane_of(p):
        size = 16 * PART_TILES[p]
        return gathered.at[pl.ds(PART_BASE[p] + (core * 4 + pos[ORDERS[p][2]]) * size, size)]

    def list_block(phase):
        first = core * 64 + pos[2] * 16
        if phase < 2:
            first = first + pos[1] * 4
        if phase < 1:
            first = first + pos[0]
        return lists.at[pl.ds(first, 4**phase)]

    done = 0
    for p in range(3):
        own = chunk(p)
        for i in range(PART_TILES[p]):
            own[i] = tiles[done + i]
        done += PART_TILES[p]
    list_block(0)[0] = slist

    def spread(ref, axis, sems, n):
        return {
            off: put(ref, ref, sems[0].at[n + k], sems[1].at[n + k], shifted(axis, off))
            for k, off in enumerate(OFFSETS)
        }

    def spread_list(phase):
        return spread(list_block(phase), phase, (list_send, list_recv), 3 * phase)

    def arrive(copies):
        for copy in copies.values():
            copy.wait_recv()

    sib_copies = []

    def to_sibling(ref):
        n = len(sib_copies)
        sib_copies.append(put(ref, ref, sib_send.at[n], sib_recv.at[n], sibling))

    phase3 = {}

    def start3(p, k2):
        axis = ORDERS[p][2]
        ref = rows_of(p, k2, 0)
        n = (p * 4 + k2) * 3
        phase3[p, k2] = copies = []
        if k2 not in RELAY_UP + RELAY_DOWN:
            copies.append(put(ref, ref, p3_send.at[n], p3_recv.at[n], shifted(axis, 2)))
        copies.append(put(ref, ref, p3_send.at[n + 1], p3_recv.at[n + 1], shifted(axis, 1)))
        copies.append(put(ref, ref, p3_send.at[n + 2], p3_recv.at[n + 2], shifted(axis, 3)))

    def relay3(k2):
        if k2 not in RELAY_UP + RELAY_DOWN:
            for p in range(3):
                phase3[p, k2][1].wait_recv()
                phase3[p, k2][2].wait_recv()
            return
        up = k2 in RELAY_UP
        for p in range(3):
            axis = ORDERS[p][2]
            n = (p * 4 + k2) * 3
            phase3[p, k2][0 if up else 1].wait_recv()
            ref = rows_of(p, k2, 3 if up else 1)
            copy = put(ref, ref, p3_send.at[n], p3_recv.at[n], shifted(axis, 1 if up else 3))
            phase3[p, k2].insert(0, copy)
        for p in range(3):
            phase3[p, k2][2 if up else 1].wait_recv()

    phase1 = [spread(chunk(p), ORDERS[p][0], (p1_send, p1_recv), 3 * p) for p in range(3)]
    lists1 = spread_list(0)

    mid = win.at[pl.ds(CPD, CPD)]
    halo = [
        put(mid, win.at[pl.ds(0, CPD)], halo_send.at[0], halo_recv.at[0], neighbour(1)),
        put(mid, win.at[pl.ds(2 * CPD, CPD)], halo_send.at[1], halo_recv.at[1], neighbour(127)),
    ]

    loads["ncol"].wait()
    wanted = ncol_v[...] - (me - 1) * CPD
    wanted = jnp.where(wanted < 0, wanted + NCL, wanted)
    wanted = jnp.where(wanted >= NCL, wanted - NCL, wanted)
    ncol_v[...] = jnp.clip(wanted, 0, 3 * CPD - 1)
    loads["far"].wait()
    q = far_v[...]
    src = (q * 43691) >> 19
    slot = q - src * CAP
    src_g, src_s = src >> 4, src & 15
    order = (src_g & 1) * 64 + (src_s >> 2) * 16 + (src_g >> 1) * 4 + (src_s & 3)
    far_v[...] = jnp.clip(order * 16 + slot, 0, 2047)
    ncol_copy = pltpu.make_async_copy(ncol_v, ncol_s, smem_sem.at[0])
    far_copy = pltpu.make_async_copy(far_v, far_s, smem_sem.at[1])
    ncol_copy.start()
    far_copy.start()

    loads["pc"].wait()
    loads["prev"].wait()
    pc = pc_v[...]
    pc_hi, pc_lo = split(pc)
    pc_rows = jnp.concatenate([pc_hi, pc_hi], axis=1)
    pc_rows2 = jnp.concatenate([pc_lo, pc_lo], axis=1)
    pc_all = jnp.concatenate([pc_rows, pc_rows2], axis=0)

    def previous_step(c, _):
        cols = pl.ds(pl.multiple_of(c * 512, 512), 512)
        hi, lo = split(prev_v[:, cols])
        both = nn(pc_all, jnp.concatenate([hi, lo], axis=0))
        vbuf[:, cols] = both[0:16] + both[16:32]
        return 0

    lax.fori_loop(0, ROWS // 512, previous_step, 0)

    for copies in phase1:
        arrive(copies)
    arrive(lists1)
    lists2 = spread_list(1)
    phase2 = [spread(rows_of(p, 0, 0), ORDERS[p][1], (p2_send, p2_recv), 3 * p) for p in range(3)]
    for p in range(3):
        start3(p, 0)
    loads["mass"].wait()
    loads["coup"].wait()
    ncol_copy.wait()
    far_copy.wait()
    arrive(lists2)
    lists3 = spread_list(2)
    for k2, off in ((1, 3), (3, 1), (2, 2)):
        if k2 == 2:
            relay3(0)
        for p in range(3):
            phase2[p][off].wait_recv()
            start3(p, k2)
    for p in range(3):
        to_sibling(plane_of(p))

    for copy in halo:
        copy.wait_recv()

    def near_step(r, _):
        xs, ms = [], []
        for j in range(NNEAR):
            w = ncol_s[j, r]
            xs.append(win[w])
        x = jnp.concatenate(xs, axis=1)
        m = near_v[pl.ds(r * NNEAR, NNEAR)]
        m = jnp.concatenate([m[j] for j in range(NNEAR)], axis=1)
        cols = pl.ds(pl.multiple_of(r * CL, CL), CL)
        ibuf[:, cols] = nt(x, m) + mass_v[pl.ds(r, 1), :] * cur_v[:, cols]
        return 0

    def near_chunk(n):
        rows_per = CPD // NEAR_CHUNKS
        near_loads[n].wait()
        lax.fori_loop(n * rows_per, (n + 1) * rows_per, near_step, 0, unroll=8)

    def forward3(k2):
        for p in range(3):
            to_sibling(rows_of(p, k2, 1))
            to_sibling(rows_of(p, k2, 3))

    near_chunk(0)
    arrive(lists3)
    list_plane = lists.at[pl.ds(core * 64, 64)]
    list_sib = put(list_plane, list_plane, list_send.at[9], list_recv.at[9], sibling)
    near_chunk(1)
    relay3(1)
    forward3(0)
    forward3(1)
    near_chunk(2)
    near_chunk(3)
    relay3(3)
    forward3(3)
    near_chunk(4)
    list_sib.wait_recv()

    mine = (lax.broadcasted_iota(jnp.int32, (16, 128), 1) == me).astype(BF)
    local = nt(mine, lists[...].reshape(2048, 128))[0:1]
    local = jnp.clip(local.astype(jnp.int32), 0, CPD - 1)
    t = lax.broadcasted_iota(jnp.int32, (1, 2048), 1) >> 4
    sx, sy, sz, sc = t & 3, (t >> 2) & 3, (t >> 4) & 3, t >> 6
    tile = (local * 13) >> 6
    at_a = (((sc * 4 + sz) * 4 + sy) * 4 + sx) * 3 + tile
    at_b = PART_BASE[1] + (((sc * 4 + sy) * 4 + sx) * 4 + sz) * 4 + tile - 3
    at_c = PART_BASE[2] + (((sc * 4 + sx) * 4 + sz) * 4 + sy) * 3 + tile - 7
    at = jnp.where(tile < 3, at_a, jnp.where(tile < 7, at_b, at_c))
    turn = (128 - (local - tile * PER_TILE) * RANK) & 127
    addr_v[...] = jnp.clip(at, 0, TILES - 1) * 128 + turn
    addr_copy = pltpu.make_async_copy(addr_v, addr_s, smem_sem.at[2])
    addr_copy.start()
    near_chunk(5)
    relay3(2)
    forward3(2)
    for k2 in (0, 1, 3, 2):
        for p in range(3):
            phase3[p, k2][0].wait_recv()
            to_sibling(rows_of(p, k2, 2))
    addr_copy.wait()
    for copy in sib_copies:
        copy.wait_recv()

    lane = lax.broadcasted_iota(jnp.int32, (16, 128), 1)
    diag = lax.broadcasted_iota(jnp.int32, (128, 8 * RANK), 0) // NRHS == (
        lax.broadcasted_iota(jnp.int32, (128, 8 * RANK), 1) // RANK
    )

    def far_step(i, total):
        for u in range(FAR_UNROLL):
            g = i * FAR_UNROLL + u
            for r in range(8):
                row = [None] * 6
                for j in range(NFAR):
                    word = addr_s[0, far_s[j, g * 8 + r]]
                    tile = pltpu.roll(gathered[word >> 7], (word + j * RANK) & 127, 1)
                    k, first = j * RANK // 128, j * RANK % 128
                    row[k] = tile if first == 0 else jnp.where(lane >= first, tile, row[k])
                    if first + RANK > 128:
                        row[k + 1] = tile
                xbuf[u, r * 16 : r * 16 + 16, :] = jnp.concatenate(row, axis=1)
            rows = pl.ds(pl.multiple_of(g * 192, 192), 192)
            combined = nt(xbuf[u], coup_v[rows, :])
            combined = jnp.where(diag, combined, 0.0).astype(BF)
            far = nn(combined, basis_v[rows, :])
            cols = pl.ds(pl.multiple_of(g * 1024, 1024), 1024)
            far = jnp.concatenate([far[r * 16 : r * 16 + 16] for r in range(8)], axis=1)
            image = ibuf[:, cols] + far
            j_hi, j_lo = split(image - vbuf[:, cols])
            i_hi, i_lo = split(image)
            stack[0:16, cols] = j_hi
            stack[16:32, cols] = j_lo
            s = jnp.concatenate([j_hi, j_lo, stack[32:64, cols]], axis=0)
            total = total + nt(s, jnp.concatenate([s, i_hi, i_lo], axis=0))
        return total

    inner = lax.fori_loop(0, NGRP // FAR_UNROLL, far_step, jnp.zeros((64, 96), F32))
    stack_copy = pltpu.make_async_copy(stack, stack_h, out_sem)
    stack_copy.start()

    inner = jnp.concatenate([inner, jnp.zeros((64, 32), F32)], axis=1)
    inner = inner + pltpu.roll(inner, 112, 1)
    j_rows = inner[0:16] + inner[16:32]
    c_rows = inner[32:48] + inner[48:64]
    mixed = jnp.where(lane < 48, c_rows, pltpu.roll(c_rows, 112, 1))
    mixed = jnp.where(lane < 32, pltpu.roll(c_rows, 16, 1), mixed)
    mixed = jnp.where(lane < 16, j_rows, mixed)
    mixed = jnp.where(lane[0:8] < 64, mixed[0:8], pltpu.roll(mixed[8:16], 64, 1))

    def reduce(value, buf, place_at, devices, n):
        buf[place_at] = value
        ref = buf.at[place_at]
        copies = [
            put(ref, ref, red_send.at[n + k], red_recv.at[n + k], d) for k, d in enumerate(devices)
        ]
        for copy in copies:
            copy.wait_recv()
        parts = [buf[k] for k in range(len(devices) + 1)]
        while len(parts) > 1:
            parts = [a + b for a, b in zip(parts[::2], parts[1::2])]
        return parts[0]

    mixed = reduce(mixed, red_a, pos[0] * 2 + core, [at_xc(*o) for o in XC], 0)
    mixed = reduce(mixed, red_b, pos[1] * 4 + pos[2], [at_yz(*o) for o in YZ], 7)
    mixed_ref[...] = mixed * (1.0 / N)
    stack_copy.wait()
    for copy in sends:
        copy.wait_send()


def finish(stack_h, mixed_ref, out_h, proj_ref, tri_ref, stack, out_v, load_sem, out_sem):
    third = ROWS // 3
    loads = []
    for n in range(3):
        part = pl.ds(n * third, third)
        loads.append(
            pltpu.make_async_copy(stack_h.at[:, part], stack.at[:, part], load_sem.at[n])
        )
        loads[n].start()
    mixed = mixed_ref[...]
    mixed = jnp.concatenate([mixed, pltpu.roll(mixed, 64, 1)], axis=0)
    row_id = lax.broadcasted_iota(jnp.int32, (16, 128), 0)
    lane_id = lax.broadcasted_iota(jnp.int32, (16, 128), 1)
    jj, cj, cc, proj = mixed[:, 0:16], mixed[:, 16:32], mixed[:, 32:48], mixed[:, 48:64]
    proj_ref[...] = proj
    left = jnp.concatenate([proj, cj], axis=0)
    right = jnp.concatenate([cj - nn(cc, proj, HIGHEST), proj], axis=0)
    gram = jj - tn(left, right, HIGHEST)

    eye = (lane_id[:, 0:16] == row_id[:, 0:16]).astype(F32)
    minus = -proj.T
    m = jnp.concatenate([gram, eye, eye, minus, minus, jnp.zeros((16, 48), F32)], axis=1)
    for k in range(16):
        pivot_row = jnp.broadcast_to(m[k : k + 1, :], (16, 128))
        pivot = m[k : k + 1, k : k + 1]
        factor = jnp.broadcast_to(m[:, k : k + 1] / pivot, (16, 128))
        m = m - jnp.where(row_id > k, factor, 0.0) * pivot_row
    d = jnp.sum(jnp.where(lane_id == row_id, m, 0.0), axis=1, keepdims=True)
    m = m / jnp.sqrt(d)
    upper = jnp.where(lane_id[:, 0:16] >= row_id[:, 0:16], m[:, 0:16], 0.0)
    tri_ref[...] = upper.T
    hi, lo = split(m[:, 16:80])
    lhs = jnp.concatenate([hi, lo], axis=0)

    def out_step(c, _):
        cols = pl.ds(pl.multiple_of(c * 1024, 1024), 1024)
        both = nn(lhs, stack[:, cols])
        out_v[:, cols] = both[0:16] + both[16:32]
        return 0

    stores = []
    for n in range(3):
        part = pl.ds(n * third, third)
        loads[n].wait()
        lax.fori_loop(n * 2, n * 2 + 2, out_step, 0, unroll=2)
        stores.append(pltpu.make_async_copy(out_v.at[:, part], out_h.at[:, part], out_sem.at[n]))
        stores[n].start()
    for copy in stores:
        copy.wait()


def per_device(
    current, previous, prev_coupling, mass_diag, near_blocks, near_cols,
    cluster_basis, coupling, send_list, far_slot,
):
    dma = pltpu.SemaphoreType.DMA
    vmem = pl.BlockSpec(memory_space=pltpu.VMEM)
    hbm = pl.BlockSpec(memory_space=pl.ANY)
    stack, mixed = pl.pallas_call(
        kernel,
        out_shape=(
            jax.ShapeDtypeStruct((64, ROWS), BF),
            jax.ShapeDtypeStruct((8, 128), F32),
        ),
        in_specs=[hbm] * 10,
        out_specs=(hbm, vmem),
        scratch_shapes=[
            pltpu.VMEM((NRHS, ROWS), F32),
            pltpu.VMEM((NRHS, ROWS), F32),
            pltpu.VMEM((NRHS, NRHS), F32),
            pltpu.VMEM((CPD, CL), F32),
            pltpu.VMEM((CPD * NNEAR, CL, CL), BF),
            pltpu.VMEM((CPD * RANK, CL), BF),
            pltpu.VMEM((CPD * RANK, NFAR * RANK), BF),
            pltpu.VMEM((CAP, 1, 128), jnp.int32),
            pltpu.VMEM((NNEAR, CPD), jnp.int32),
            pltpu.VMEM((NFAR, CPD), jnp.int32),
            pltpu.VMEM((3 * CPD, NRHS, CL), BF),
            pltpu.VMEM((64, ROWS), BF),
            pltpu.VMEM((NRHS, ROWS), F32),
            pltpu.VMEM((NRHS, ROWS), F32),
            pltpu.VMEM((TILES, NRHS, 128), BF),
            pltpu.VMEM((128, NRHS, 128), BF),
            pltpu.VMEM((FAR_UNROLL, 128, NFAR * RANK), BF),
            pltpu.VMEM((1, 2048), jnp.int32),
            pltpu.SMEM((NNEAR, CPD), jnp.int32),
            pltpu.SMEM((NFAR, CPD), jnp.int32),
            pltpu.SMEM((1, 2048), jnp.int32),
            pltpu.VMEM((8, 8, 128), F32),
            pltpu.VMEM((16, 8, 128), F32),
            dma((9,)),
            dma((NEAR_CHUNKS,)),
            dma((3,)),
            dma,
            dma((9,)),
            dma((9,)),
            dma((9,)),
            dma((9,)),
            dma((36,)),
            dma((36,)),
            dma((10,)),
            dma((10,)),
            dma((39,)),
            dma((39,)),
            dma((2,)),
            dma((2,)),
            dma((22,)),
            dma((22,)),
        ],
        compiler_params=pltpu.CompilerParams(
            collective_id=0, has_side_effects=True, vmem_limit_bytes=56 << 20
        ),
    )(
        current,
        previous,
        prev_coupling,
        mass_diag.reshape(CPD, CL),
        near_blocks.reshape(CPD * NNEAR, CL, CL),
        near_cols.T,
        cluster_basis.reshape(CPD * RANK, CL),
        coupling.reshape(CPD * RANK, NFAR * RANK),
        send_list.transpose(2, 0, 1),
        far_slot.T,
    )
    return pl.pallas_call(
        finish,
        out_shape=(
            jax.ShapeDtypeStruct((NRHS, ROWS), F32),
            jax.ShapeDtypeStruct((NRHS, NRHS), F32),
            jax.ShapeDtypeStruct((NRHS, NRHS), F32),
        ),
        in_specs=[hbm, vmem],
        out_specs=(hbm, vmem, vmem),
        scratch_shapes=[
            pltpu.VMEM((64, ROWS), BF),
            pltpu.VMEM((NRHS, ROWS), F32),
            dma((3,)),
            dma((3,)),
        ],
    )(stack, mixed)


def solution(mesh):
    placed = (
        P(None, ("group", "sub")),
        P(None, ("group", "sub")),
        P(),
        P(("group", "sub")),
        P(("group", "sub"), None, None, None),
        P(("group", "sub"), None),
        P(("group", "sub"), None, None),
        P(("group", "sub"), None, None),
        P(("group", "sub"), None, None),
        P(("group", "sub"), None),
    )
    return jax.shard_map(
        per_device,
        mesh=mesh,
        in_specs=placed,
        out_specs=(P(None, ("group", "sub")), P(), P()),
        check_vma=False,
    )
```
